32 devices in a mesh: layer: 4 (over z), row: 4 (over y, x), col: 2 (over core).
Axes of the slice: x: 2, y: 2, z: 4, core: 2. Of those that a mesh axis runs over, the one named last changes fastest.
Arguments:
- leaf_rhs: float32 [4, 3, 1024, 256], P('layer', None, 'row'), may hold values from -6 to 6
- anc_rhs: float32 [2, 1024, 256], P(None, 'row'), may hold values from -6 to 6
- leaf_tiles: bfloat16 [4, 3, 1024, 1024], P('layer', None, 'row', 'col'), may hold values from -0.1875 to 0.1875
- cross_tiles: bfloat16 [4, 2, 3, 1024, 1024], P('layer', None, None, 'row', 'col'), may hold values from -0.09375 to 0.09375
- top_tiles: bfloat16 [1, 1024, 1024], P(None, 'row', 'col'), may hold values from -0.1875 to 0.1875
- leaf_pattern: int32 [4, 3, 8, 8], P('layer', None, 'row', 'col'), may hold values 0 or 1
- cross_pattern: int32 [4, 2, 3, 8, 8], P('layer', None, None, 'row', 'col'), may hold values 0 or 1
- top_pattern: int32 [1, 8, 8], P(None, 'row', 'col'), may hold values 0 or 1
- leaf_inverse: bfloat16 [4, 3, 8, 128, 128], P('layer'), may hold values from -0.5 to 0.5
- anc_inverse: bfloat16 [2, 8, 128, 128], replicated, may hold values from -0.5 to 0.5
Outputs:
- leaf_solution: bfloat16 [4, 3, 1024, 256], P('layer', None, 'row')
- anc_solution: bfloat16 [2, 1024, 256], P(None, 'row')
The draws below stay inside these ranges and needn't reach their ends.
All inputs are finite; a program needn't handle non-finite values. No bound on the sum of `leaf_pattern` or of `cross_pattern` or of `top_pattern` on one device may be relied on, other than what follows from the above.
Results may differ from the reference program's by a relative error of at most 0.023.
Values may be sent and summed in bfloat16 or wider, within the bound.
A program may use at most 128 MiB of HBM per device.

```python
import jax
import jax.numpy as jnp
from jax import lax

TILE = 128
NRHS = 256
LEAF_LEV = 3
ANC_LEV = 2
NSUP = 8
NODES = 1024
LEAF_PAIRS = 3
ANC_PAIRS = 1
N_LAYER = 4


def set_ends(drawn, stream_key, low, top_value):
    longest = drawn.shape.index(max(drawn.shape))
    spots = []
    for shift in (0, 1):
        where = [jax.random.randint(jax.random.fold_in(stream_key, axis), (), 0, length) for axis, length in enumerate(drawn.shape)]
        where[longest] = (where[longest] + shift) % drawn.shape[longest]
        spots.append(tuple(where))
    return drawn.at[spots[0]].set(low).at[spots[1]].set(top_value)


def shard_levels(own_key, dims, cuts, least, top_value):
    def one(dim, parts):
        steps = jax.random.uniform(jax.random.fold_in(jax.random.fold_in(own_key, 6), dim), (parts,), jnp.float32, least / len(cuts), top_value / len(cuts))
        return jnp.repeat(jnp.exp(steps), dims[dim] // parts).reshape((-1,) + (1,) * (len(dims) - dim - 1))

    loudness = one(*cuts[0])
    for cut in cuts[1:]:
        loudness = loudness * one(*cut)
    return loudness


def normal_values(rng, dims, deviation, bound, cuts=(), held_as=jnp.bfloat16):
    values = deviation * jax.random.normal(rng, dims, jnp.float32)
    if cuts:
        values = values * shard_levels(rng, dims, cuts, -0.22, 0.18)
    return jnp.clip(values, -bound, bound).astype(held_as)


def setup_inputs(seed: int = 0) -> dict:
    key_of = jax.random.split(jax.random.key(seed), 11)
    return {
        "leaf_rhs": normal_values(key_of[0], (N_LAYER, LEAF_LEV, NODES, NRHS), 1.0, 6.0, ((0, 4), (2, 4)), jnp.float32),
        "anc_rhs": normal_values(key_of[1], (ANC_LEV, NODES, NRHS), 1.0, 6.0, ((1, 4),), jnp.float32),
        "leaf_tiles": normal_values(key_of[2], (N_LAYER, LEAF_PAIRS, NODES, NODES), NODES ** -0.5, 0.1875, ((0, 4), (2, 4), (3, 2))),
        "cross_tiles": normal_values(key_of[3], (N_LAYER, ANC_LEV, LEAF_LEV, NODES, NODES), (NODES * N_LAYER) ** -0.5, 0.09375, ((0, 4), (3, 4), (4, 2))),
        "top_tiles": normal_values(key_of[4], (ANC_PAIRS, NODES, NODES), NODES ** -0.5, 0.1875, ((1, 4), (2, 2))),
        "leaf_pattern": set_ends((jax.random.randint(key_of[5], (N_LAYER, LEAF_PAIRS, NSUP, NSUP), 0, 2) < 1).astype(jnp.int32), jax.random.fold_in(key_of[5], 1), 0, 1),
        "cross_pattern": set_ends((jax.random.randint(key_of[6], (N_LAYER, ANC_LEV, LEAF_LEV, NSUP, NSUP), 0, 2) < 1).astype(jnp.int32), jax.random.fold_in(key_of[6], 1), 0, 1),
        "top_pattern": set_ends((jax.random.randint(key_of[7], (ANC_PAIRS, NSUP, NSUP), 0, 2) < 1).astype(jnp.int32), jax.random.fold_in(key_of[7], 1), 0, 1),
        "leaf_inverse": normal_values(key_of[8], (N_LAYER, LEAF_LEV, NSUP, TILE, TILE), TILE ** -0.5, 0.5, ((0, 4),)),
        "anc_inverse": normal_values(key_of[9], (ANC_LEV, NSUP, TILE, TILE), TILE ** -0.5, 0.5),
    }


def pair_index(target, source):
    return target * (target - 1) // 2 + source


def product(pattern, tiles, vector, flipped):
    grown = jnp.repeat(jnp.repeat(pattern, TILE, axis=0), TILE, axis=1)
    dense = (tiles * grown.astype(tiles.dtype)).astype(jnp.float32)
    values = vector.astype(jnp.float32)
    if flipped:
        return jnp.dot(dense.T, values, precision=lax.Precision.HIGHEST)
    return jnp.dot(dense, values, precision=lax.Precision.HIGHEST)


def solve_blocks(inverse, residual, flipped):
    rounded = lax.optimization_barrier(residual.astype(jnp.bfloat16))
    pieces = rounded.astype(jnp.float32).reshape(NSUP, TILE, NRHS)
    text_form = "sji,sjk->sik" if flipped else "sij,sjk->sik"
    solved = jnp.einsum(text_form, inverse.astype(jnp.float32), pieces, precision=lax.Precision.HIGHEST)
    return solved.reshape(NODES, NRHS).astype(jnp.bfloat16)


def reference(leaf_rhs, anc_rhs, leaf_tiles, cross_tiles, top_tiles, leaf_pattern, cross_pattern, top_pattern, leaf_inverse, anc_inverse):
    layer_total = leaf_rhs.shape[0]
    forward_leaf = []
    for layer_number in range(layer_total):
        solved_levels = []
        for target in range(LEAF_LEV):
            summed = jnp.zeros((NODES, NRHS), jnp.float32)
            for source in range(target):
                pair_slot = pair_index(target, source)
                summed = summed + product(leaf_pattern[layer_number, pair_slot], leaf_tiles[layer_number, pair_slot], solved_levels[source], False)
            solved_levels.append(solve_blocks(leaf_inverse[layer_number, target], leaf_rhs[layer_number, target] - summed, False))
        forward_leaf.append(solved_levels)
    forward_anc = []
    for target in range(ANC_LEV):
        summed = jnp.zeros((NODES, NRHS), jnp.float32)
        for layer_number in range(layer_total):
            for source in range(LEAF_LEV):
                summed = summed + product(cross_pattern[layer_number, target, source], cross_tiles[layer_number, target, source], forward_leaf[layer_number][source], False)
        for source in range(target):
            pair_slot = pair_index(target, source)
            summed = summed + product(top_pattern[pair_slot], top_tiles[pair_slot], forward_anc[source], False)
        forward_anc.append(solve_blocks(anc_inverse[target], anc_rhs[target] - summed, False))
    anc_out = [None] * ANC_LEV
    for target in range(ANC_LEV - 1, -1, -1):
        summed = jnp.zeros((NODES, NRHS), jnp.float32)
        for source in range(target + 1, ANC_LEV):
            pair_slot = pair_index(source, target)
            summed = summed + product(top_pattern[pair_slot], top_tiles[pair_slot], anc_out[source], True)
        anc_out[target] = solve_blocks(anc_inverse[target], forward_anc[target].astype(jnp.float32) - summed, True)
    leaf_out = []
    for layer_number in range(layer_total):
        level_out = [None] * LEAF_LEV
        for target in range(LEAF_LEV - 1, -1, -1):
            summed = jnp.zeros((NODES, NRHS), jnp.float32)
            for upper in range(ANC_LEV):
                summed = summed + product(cross_pattern[layer_number, upper, target], cross_tiles[layer_number, upper, target], anc_out[upper], True)
            for source in range(target + 1, LEAF_LEV):
                pair_slot = pair_index(source, target)
                summed = summed + product(leaf_pattern[layer_number, pair_slot], leaf_tiles[layer_number, pair_slot], level_out[source], True)
            level_out[target] = solve_blocks(leaf_inverse[layer_number, target], forward_leaf[layer_number][target].astype(jnp.float32) - summed, True)
        leaf_out.append(jnp.stack(level_out))
    return jnp.stack(leaf_out), jnp.stack(anc_out)
```

```python
import functools

import jax
import jax.numpy as jnp
from jax import lax
from jax.experimental import pallas as pl
from jax.experimental.pallas import tpu as pltpu
from jax.sharding import PartitionSpec as P

MESH = pl.DeviceIdType.MESH
NT = (((1,), (1,)), ((), ()))
NN = (((1,), (0,)), ((), ()))
F32 = jnp.float32
BF16 = jnp.bfloat16


def pair_index(target, source):
    return target * (target - 1) // 2 + source


def dot(left, right, form):
    return lax.dot_general(left, right, form, preferred_element_type=F32)


def loop(start, stop, body, init):
    if stop - start <= 4:
        carry = init
        for index in range(start, stop):
            carry = body(index, carry)
        return carry
    return lax.fori_loop(start, stop, body, init)


def solve(inverse, level, residual, flipped):
    wide = inverse.shape[-1]
    pieces = []
    rounded = residual.astype(BF16)
    for block in range(inverse.shape[1]):
        part = rounded[:, block * wide : (block + 1) * wide]
        pieces.append(dot(part, inverse[level, block], NN if flipped else NT))
    return jnp.concatenate(pieces, axis=1)


def kernel(
    dims,
    leaf_rhs, anc_rhs, leaf_tiles, cross_tiles, top_tiles,
    leaf_pat, cross_pat, top_pat, leaf_inv, anc_inv,
    leaf_out, anc_out,
    rhs_in, arhs_in, inv, ainv, rhs_t, arhs_t, leaf_m, cross_m, top_m,
    ybuf, fsum, csum, zs, zr, zbuf, xanc, asend, arecv,
    bsum, bown, bsend, brecv, xbuf, stage,
    load_sem, col_ssem, col_rsem, y_ssem, y_rsem, z_ssem, z_rsem,
    lrs_ssem, lrs_rsem, lag_ssem, lag_rsem, a_ssem, a_rsem, b_ssem, b_rsem,
    out_sem, out_ssem, out_rsem,
):
    R, L, C, Q, T, A, B, H, HQ, HL, W = dims
    RC = R // C
    LQ = L // Q
    SB = B // W
    LP = T * (T - 1) // 2
    AP = A * (A - 1) // 2
    row = lax.axis_index("row")
    layer = lax.axis_index("layer")
    col = lax.axis_index("col")

    def ahead(axis_index, step, size):
        return lax.rem(axis_index + step, size)

    def behind(axis_index, step, size):
        return lax.rem(axis_index + size - step, size)

    loads = []

    def load(src, dst):
        copy = pltpu.make_async_copy(src, dst, load_sem.at[len(loads)])
        copy.start()
        loads.append(copy)
        return copy

    my_cols = pl.ds(pl.multiple_of(col * H, H), H)
    ld_rhs = [load(leaf_rhs.at[0, 0, :, my_cols], rhs_in.at[0])]
    ld_inv = load(leaf_inv.at[0, :, pl.ds(row * SB, SB)], inv)
    ld_leaf = [
        load(leaf_tiles.at[0, :, :, pl.ds(j * B, B)], leaf_m.at[:, col * RC + j])
        for j in range(RC)
    ]
    for t in range(1, T):
        ld_rhs.append(load(leaf_rhs.at[0, t, :, my_cols], rhs_in.at[t]))
    ld_cross = [
        load(cross_tiles.at[0, :, :, :, pl.ds(j * B, B)], cross_m.at[:, :, col * RC + j])
        for j in range(RC)
    ]
    ld_top = [
        load(top_tiles.at[:, :, pl.ds(j * B, B)], top_m.at[:, col * RC + j])
        for j in range(RC)
    ]
    ld_arhs = load(anc_rhs.at[:, :, my_cols], arhs_in)
    ld_ainv = load(anc_inv.at[:, pl.ds(row * SB, SB)], ainv)

    barrier = pltpu.get_barrier_semaphore()
    for name, mine, size in (("row", row, R), ("layer", layer, L), ("col", col, C)):
        for step in range(1, size):
            pl.semaphore_signal(
                barrier, inc=1, device_id={name: ahead(mine, step, size)}, device_id_type=MESH
            )

    def remote(src, dst, ssem, rsem, name, target):
        return pltpu.make_async_remote_copy(
            src_ref=src, dst_ref=dst, send_sem=ssem, recv_sem=rsem,
            device_id={name: target}, device_id_type=MESH,
        )

    def y_copy(t, q, k, source):
        block = ybuf.at[t, q, source]
        return remote(block, block, y_ssem.at[t, q, k], y_rsem.at[t, q, k], "row", ahead(row, k, R))

    def z_copy(a, k, source):
        block = zbuf.at[a, source]
        return remote(block, block, z_ssem.at[a, k], z_rsem.at[a, k], "row", ahead(row, k, R))

    def a_copy(a, k):
        return remote(
            asend.at[a, k], arecv.at[a, k], a_ssem.at[a, k], a_rsem.at[a, k], "row", ahead(row, k, R)
        )

    def b_copy(t, q, k):
        return remote(
            bsend.at[t, q, k], brecv.at[t, q, k], b_ssem.at[t, q, k], b_rsem.at[t, q, k],
            "row", ahead(row, k, R),
        )

    def lrs_copy(k):
        target = ahead(layer, k, L)
        return remote(zs.at[target], zr.at[k], lrs_ssem.at[k], lrs_rsem.at[k], "layer", target)

    def lag_copy(a, k, source):
        block = xanc.at[a, source]
        return remote(
            block, block, lag_ssem.at[a, k], lag_rsem.at[a, k], "layer", ahead(layer, k, L)
        )

    def tile_copy(slot, k, source):
        held = pl.ds(source * RC, RC)
        if slot < LP:
            block = leaf_m.at[slot, held]
        elif slot < LP + A * T:
            block = cross_m.at[(slot - LP) // T, (slot - LP) % T, held]
        else:
            block = top_m.at[slot - LP - A * T, held]
        return remote(
            block, block, col_ssem.at[slot, k], col_rsem.at[slot, k], "col", ahead(col, k, C)
        )

    def tiles_arrive(slot):
        for k in range(1, C):
            tile_copy(slot, k, behind(col, k, C)).wait_recv()

    def send_tiles(slot):
        for k in range(1, C):
            tile_copy(slot, k, col).start()

    def each(start, stop, action):
        def body(index, carry):
            action(index)
            return carry

        loop(start, stop, body, 0)

    def mask(ref, lead, pattern, lead_pattern):
        def one(j):
            for i in range(SB):
                for n in range(SB):
                    bit = pattern[(*lead_pattern, i, j * SB + n)].astype(F32)
                    spread = jnp.full((W, W), bit, F32).astype(BF16)
                    at = (*lead, col * RC + j, pl.ds(i * W, W), pl.ds(n * W, W))
                    ref[at] = ref[at] * spread

        each(0, RC, one)

    def send_y(t, q):
        each(1, R, lambda k: y_copy(t, q, k, row).start())

    def turn_rhs(t):
        ld_rhs[t].wait()
        rhs_t[t] = rhs_in[t].T.reshape(Q, HQ, B)

    turn_rhs(0)
    ld_inv.wait()
    for q in range(Q):
        ybuf[0, q, row] = solve(inv, 0, rhs_t[0, q], False).astype(BF16)
    pl.semaphore_wait(barrier, (R - 1) + (L - 1) + (C - 1))
    for q in range(Q):
        send_y(0, q)
    for copy in ld_leaf:
        copy.wait()
    for slot in range(LP):
        mask(leaf_m, (slot,), leaf_pat, (0, slot))
        send_tiles(slot)
    for t in range(1, T):
        turn_rhs(t)
    for copy in ld_cross:
        copy.wait()
    for a in range(A):
        for t in range(T):
            mask(cross_m, (a, t), cross_pat, (0, a, t))
            send_tiles(LP + a * T + t)
    for copy in ld_top:
        copy.wait()
    for slot in range(AP):
        mask(top_m, (slot,), top_pat, (slot,))
        send_tiles(LP + A * T + slot)
    ld_arhs.wait()
    ld_ainv.wait()
    for a in range(A):
        arhs_t[a] = arhs_in[a].T.reshape(L, HL, B)

    def product(vectors, tiles, form=NT):
        return loop(
            1, R,
            lambda k, total: total + dot(vectors(k), tiles(k), form),
            dot(vectors(0), tiles(0), form),
        )

    arrived = set()

    def need(slot):
        if slot not in arrived:
            arrived.add(slot)
            tiles_arrive(slot)

    zero = jnp.zeros((HQ, B), F32)

    def fold_forward(s, q):
        for t in range(s + 2, T):
            need(pair_index(t, s))
            term = product(lambda k: ybuf[s, q, k], lambda k: leaf_m[pair_index(t, s), k])
            fsum[t, q] = term if s == 0 else fsum[t, q] + term
        for a in range(A):
            need(LP + a * T + s)
            term = product(lambda k: ybuf[s, q, k], lambda k: cross_m[a, s, k])
            here = pl.ds(q * LQ, LQ)
            if s > 0:
                term = term + csum[a, here].reshape(HQ, B)
            csum[a, here] = term.reshape(LQ, HL, B)

    for t in range(1, T):
        for q in range(Q):
            need(pair_index(t, t - 1))

            def arriving(k, total):
                source = behind(row, k, R)
                y_copy(t - 1, q, k, source).wait_recv()
                return total + dot(ybuf[t - 1, q, source], leaf_m[pair_index(t, t - 1), source], NT)

            residual = rhs_t[t, q]
            if t > 1:
                residual = residual - fsum[t, q]
            own = dot(ybuf[t - 1, q, row], leaf_m[pair_index(t, t - 1), row], NT)
            residual = residual - loop(1, R, arriving, own)
            ybuf[t, q, row] = solve(inv, t, residual, False).astype(BF16)
            send_y(t, q)
        for q in range(Q):
            fold_forward(t - 1, q)

    last = T - 1
    for q in range(Q):
        each(1, R, lambda k: y_copy(last, q, k, behind(row, k, R)).wait_recv())
        fold_forward(last, q)
        for a in range(A):
            here = pl.ds(q * LQ, LQ)
            zs[here, a] = csum[a, here].astype(BF16)

    each(1, L, lambda k: lrs_copy(k).start())

    def add_layer(k, totals):
        lrs_copy(k).wait_recv()
        return tuple(totals[a] + zr[k, a].astype(F32) for a in range(A))

    for slot in range(AP):
        need(LP + A * T + slot)
    sums = loop(1, L, add_layer, tuple(csum[a, layer] for a in range(A)))
    for a in range(A):
        residual = arhs_t[a, layer] - sums[a]
        for s in range(a):
            if s == a - 1:
                each(1, R, lambda k: z_copy(s, k, behind(row, k, R)).wait_recv())
            residual = residual - product(
                lambda k: zbuf[s, k], lambda k: top_m[pair_index(a, s), k]
            )
        zbuf[a, row] = solve(ainv, a, residual, False).astype(BF16)
        if a < A - 1:
            each(1, R, lambda k: z_copy(a, k, row).start())
    for a in range(A - 1, -1, -1):
        residual = zbuf[a, row].astype(F32)
        if a < A - 1:

            def partial(target):
                total = None
                for b in range(a + 1, A):
                    term = dot(xanc[b, layer], top_m[pair_index(b, a), target], NN)
                    total = term if total is None else total + term
                return total

            def send_part(k):
                asend[a, k] = partial(ahead(row, k, R)).astype(BF16)
                a_copy(a, k).start()

            each(1, R, send_part)

            def add_part(k, total):
                a_copy(a, k).wait_recv()
                return total + arecv[a, k].astype(F32)

            residual = residual - loop(1, R, add_part, partial(row))
        xanc[a, layer] = solve(ainv, a, residual, True).astype(BF16)
        each(1, L, lambda k: lag_copy(a, k, layer).start())

    def out_copies(slot, k):
        if slot < T:
            held = leaf_out.at[0, slot, :, my_cols]
        else:
            held = anc_out.at[slot - T, :, my_cols]
        return remote(
            stage.at[slot], held, out_ssem.at[slot, k], out_rsem.at[slot, k], "col", ahead(col, k, C)
        )

    def out_arrival(slot, k):
        theirs = pl.ds(pl.multiple_of(behind(col, k, C) * H, H), H)
        if slot < T:
            held = leaf_out.at[0, slot, :, theirs]
        else:
            held = anc_out.at[slot - T, :, theirs]
        return remote(
            stage.at[slot], held, out_ssem.at[slot, k], out_rsem.at[slot, k], "col", ahead(col, k, C)
        )

    def out_local(slot):
        held = leaf_out.at[0, slot, :, my_cols] if slot < T else anc_out.at[slot - T, :, my_cols]
        return pltpu.make_async_copy(stage.at[slot], held, out_sem.at[slot])

    def emit(slot, value):
        stage[slot] = value.astype(F32).T.astype(BF16)
        for k in range(1, C):
            out_copies(slot, k).start()
        out_local(slot).start()

    def anc_chunk(a, q):
        return xanc[a, pl.ds(q * LQ, LQ)].reshape(HQ, B)

    def fold_cross(a, t, first):
        for q in range(Q):

            def one(k):
                term = dot(anc_chunk(a, q), cross_m[a, t, k], NN)
                bsum[t, q, k] = term if first else bsum[t, q, k] + term

            each(0, R, one)

    def start_level(t, q):
        def value(target):
            total = bsum[t, q, target]
            if t == T - 1:
                return total + dot(anc_chunk(0, q), cross_m[0, t, target], NN)
            return total + dot(xbuf[t + 1, q], leaf_m[pair_index(t + 1, t), target], NN)

        def send_part(k):
            bsend[t, q, k] = value(ahead(row, k, R)).astype(BF16)
            b_copy(t, q, k).start()

        each(1, R, send_part)
        bown[t, q] = value(row)

    for a in range(A - 1, 0, -1):
        each(1, L, lambda k: lag_copy(a, k, behind(layer, k, L)).wait_recv())
        for t in range(T - 1, -1, -1):
            fold_cross(a, t, a == A - 1)
    each(1, L, lambda k: lag_copy(0, k, behind(layer, k, L)).wait_recv())
    for q in range(Q):
        start_level(T - 1, q)
    for t in range(T - 2, -1, -1):
        fold_cross(0, t, A == 1)
    for a in range(A):
        emit(T + a, xanc[a].reshape(H, B))
    for t in range(T - 1, -1, -1):
        for q in range(Q):

            def add_part(k, total):
                b_copy(t, q, k).wait_recv()
                return total + brecv[t, q, k].astype(F32)

            residual = ybuf[t, q, row].astype(F32) - loop(1, R, add_part, bown[t, q])
            xbuf[t, q] = solve(inv, t, residual, True).astype(BF16)
            if t > 0:
                start_level(t - 1, q)
        emit(t, xbuf[t].reshape(H, B))
        for lower in range(t - 1):
            for q in range(Q):

                def one(k):
                    bsum[lower, q, k] += dot(xbuf[t, q], leaf_m[pair_index(t, lower), k], NN)

                each(0, R, one)

    for slot in range(LP + A * T + AP):
        for k in range(1, C):
            tile_copy(slot, k, col).wait_send()
    for t in range(T):
        for q in range(Q):
            each(1, R, lambda k: y_copy(t, q, k, row).wait_send())
            each(1, R, lambda k: b_copy(t, q, k).wait_send())
    for a in range(A - 1):
        each(1, R, lambda k: z_copy(a, k, row).wait_send())
        each(1, R, lambda k: a_copy(a, k).wait_send())
    each(1, L, lambda k: lrs_copy(k).wait_send())
    for a in range(A):
        each(1, L, lambda k: lag_copy(a, k, layer).wait_send())
    for slot in range(T + A):
        out_local(slot).wait()
        for k in range(1, C):
            out_copies(slot, k).wait_send()
            out_arrival(slot, k).wait_recv()


def local(R, L, C, *arrays):
    leaf_rhs, anc_rhs = arrays[:2]
    T = leaf_rhs.shape[1]
    A = anc_rhs.shape[0]
    B = leaf_rhs.shape[2]
    H = leaf_rhs.shape[3] // C
    W = arrays[8].shape[-1]
    Q = 2 if R <= 4 and L % 2 == 0 else 1
    HQ, HL = H // Q, H // L
    SB = B // W
    LP, AP = T * (T - 1) // 2, A * (A - 1) // 2
    dims = (R, L, C, Q, T, A, B, H, HQ, HL, W)
    vmem = pltpu.VMEM
    dma = pltpu.SemaphoreType.DMA
    slots = LP + A * T + AP
    scratch = [
        vmem((T, B, H), F32), vmem((A, B, H), F32),
        vmem((T, SB, W, W), BF16), vmem((A, SB, W, W), BF16),
        vmem((T, Q, HQ, B), F32), vmem((A, L, HL, B), F32),
        vmem((LP, R, B, B), BF16), vmem((A, T, R, B, B), BF16), vmem((AP, R, B, B), BF16),
        vmem((T, Q, R, HQ, B), BF16), vmem((T, Q, HQ, B), F32), vmem((A, L, HL, B), F32),
        vmem((L, A, HL, B), BF16), vmem((L, A, HL, B), BF16),
        vmem((A, R, HL, B), BF16), vmem((A, L, HL, B), BF16),
        vmem((A, R, HL, B), BF16), vmem((A, R, HL, B), BF16),
        vmem((T, Q, R, HQ, B), F32), vmem((T, Q, HQ, B), F32),
        vmem((T, Q, R, HQ, B), BF16), vmem((T, Q, R, HQ, B), BF16),
        vmem((T, Q, HQ, B), BF16), vmem((T + A, B, H), BF16),
        dma((T + 3 + 3 * (R // C),)),
        dma((slots, C)), dma((slots, C)),
        dma((T, Q, R)), dma((T, Q, R)), dma((A, R)), dma((A, R)),
        dma((L,)), dma((L,)), dma((A, L)), dma((A, L)),
        dma((A, R)), dma((A, R)), dma((T, Q, R)), dma((T, Q, R)),
        dma((T + A,)), dma((T + A, C)), dma((T + A, C)),
    ]
    anywhere = pl.BlockSpec(memory_space=pl.ANY)
    scalars = pl.BlockSpec(memory_space=pltpu.SMEM)
    return pl.pallas_call(
        functools.partial(kernel, dims),
        out_shape=(
            jax.ShapeDtypeStruct(leaf_rhs.shape, BF16),
            jax.ShapeDtypeStruct(anc_rhs.shape, BF16),
        ),
        in_specs=[anywhere] * 5 + [scalars] * 3 + [anywhere] * 2,
        out_specs=(anywhere, anywhere),
        scratch_shapes=scratch,
        compiler_params=pltpu.CompilerParams(
            collective_id=0, has_side_effects=True, vmem_limit_bytes=56 * 1024 * 1024
        ),
    )(*arrays)


def solution(mesh):
    in_specs = (
        P("layer", None, "row", None),
        P(None, "row", None),
        P("layer", None, "row", "col"),
        P("layer", None, None, "row", "col"),
        P(None, "row", "col"),
        P("layer", None, "row", "col"),
        P("layer", None, None, "row", "col"),
        P(None, "row", "col"),
        P("layer", None, None, None, None),
        P(),
    )
    out_specs = (P("layer", None, "row", None), P(None, "row", None))
    sizes = mesh.shape
    return jax.shard_map(
        functools.partial(local, sizes["row"], sizes["layer"], sizes["col"]),
        mesh=mesh, in_specs=in_specs, out_specs=out_specs, check_vma=False,
    )
```

```python
import functools

import jax
import jax.numpy as jnp
from jax import lax
from jax.experimental import pallas as pl
from jax.experimental.pallas import tpu as pltpu
from jax.sharding import PartitionSpec as P

MESH = pl.DeviceIdType.MESH
NT = (((1,), (1,)), ((), ()))
NN = (((1,), (0,)), ((), ()))
F32 = jnp.float32
BF16 = jnp.bfloat16


def pair_index(target, source):
    return target * (target - 1) // 2 + source


def dot(left, right, form):
    return lax.dot_general(left, right, form, preferred_element_type=F32)


def loop(start, stop, body, init):
    if stop - start <= 4:
        carry = init
        for index in range(start, stop):
            carry = body(index, carry)
        return carry
    return lax.fori_loop(start, stop, body, init)


def solve(inverse, level, residual, flipped):
    wide = inverse.shape[-1]
    pieces = []
    rounded = residual.astype(BF16)
    for block in range(inverse.shape[1]):
        part = rounded[:, block * wide : (block + 1) * wide]
        pieces.append(dot(part, inverse[level, block], NN if flipped else NT))
    return jnp.concatenate(pieces, axis=1)


def kernel(
    dims,
    leaf_rhs, anc_rhs, leaf_tiles, cross_tiles, top_tiles,
    leaf_pat, cross_pat, top_pat, leaf_inv, anc_inv,
    leaf_out, anc_out,
    rhs_in, arhs_in, inv, ainv, rhs_t, arhs_t, leaf_m, cross_m, top_m,
    ybuf, fsum, csum, zs, zr, zbuf, xanc, asend, arecv,
    bsum, bown, bsend, brecv, xbuf,
    load_sem, col_ssem, col_rsem, y_ssem, y_rsem, z_ssem, z_rsem,
    lrs_ssem, lrs_rsem, lag_ssem, lag_rsem, a_ssem, a_rsem, b_ssem, b_rsem,
    out_ssem, out_rsem,
):
    R, L, C, Q, T, A, B, H, HQ, HL, W = dims
    RC = R // C
    LQ = L // Q
    SB = B // W
    LP = T * (T - 1) // 2
    AP = A * (A - 1) // 2
    row = lax.axis_index("row")
    layer = lax.axis_index("layer")
    col = lax.axis_index("col")

    def ahead(axis_index, step, size):
        return lax.rem(axis_index + step, size)

    def behind(axis_index, step, size):
        return lax.rem(axis_index + size - step, size)

    binary = R & (R - 1) == 0

    def row_to(step):
        if not binary:
            return ahead(row, step, R)
        total, place = 0, 1
        while place < R:
            total = total + lax.rem(lax.div(row, place) + step // place, 2) * place
            place *= 2
        return total

    def row_from(step):
        return row_to(step) if binary else behind(row, step, R)

    loads = []

    def load(src, dst):
        copy = pltpu.make_async_copy(src, dst, load_sem.at[len(loads)])
        copy.start()
        loads.append(copy)
        return copy

    my_cols = pl.ds(pl.multiple_of(col * H, H), H)
    ld_rhs = [load(leaf_rhs.at[0, 0, :, my_cols], rhs_in.at[0])]
    ld_inv = load(leaf_inv.at[0, :, pl.ds(row * SB, SB)], inv)
    ld_leaf = [
        load(leaf_tiles.at[0, :, :, pl.ds(j * B, B)], leaf_m.at[:, col * RC + j])
        for j in range(RC)
    ]
    for t in range(1, T):
        ld_rhs.append(load(leaf_rhs.at[0, t, :, my_cols], rhs_in.at[t]))
    ld_cross = [
        load(cross_tiles.at[0, :, :, :, pl.ds(j * B, B)], cross_m.at[:, :, col * RC + j])
        for j in range(RC)
    ]
    ld_top = [
        load(top_tiles.at[:, :, pl.ds(j * B, B)], top_m.at[:, col * RC + j])
        for j in range(RC)
    ]
    ld_arhs = load(anc_rhs.at[:, :, my_cols], arhs_in)
    ld_ainv = load(anc_inv.at[:, pl.ds(row * SB, SB)], ainv)

    barrier = pltpu.get_barrier_semaphore()
    for name, mine, size in (("row", row, R), ("layer", layer, L), ("col", col, C)):
        for step in range(1, size):
            pl.semaphore_signal(
                barrier, inc=1, device_id={name: ahead(mine, step, size)}, device_id_type=MESH
            )

    def remote(src, dst, ssem, rsem, name, target):
        return pltpu.make_async_remote_copy(
            src_ref=src, dst_ref=dst, send_sem=ssem, recv_sem=rsem,
            device_id={name: target}, device_id_type=MESH,
        )

    def y_copy(t, q, k, source):
        block = ybuf.at[t, q, source]
        return remote(block, block, y_ssem.at[t, q, k], y_rsem.at[t, q, k], "row", row_to(k))

    def z_copy(a, k, source):
        block = zbuf.at[a, source]
        return remote(block, block, z_ssem.at[a, k], z_rsem.at[a, k], "row", row_to(k))

    def a_copy(a, k):
        return remote(
            asend.at[a, k], arecv.at[a, k], a_ssem.at[a, k], a_rsem.at[a, k], "row", row_to(k)
        )

    def b_copy(t, q, k):
        return remote(
            bsend.at[t, q, k], brecv.at[t, q, k], b_ssem.at[t, q, k], b_rsem.at[t, q, k],
            "row", row_to(k),
        )

    def lrs_copy(a, k):
        target = ahead(layer, k, L)
        return remote(
            zs.at[a, target], zr.at[a, k], lrs_ssem.at[a, k], lrs_rsem.at[a, k], "layer", target
        )

    def lag_copy(a, k, source):
        block = xanc.at[a, source]
        return remote(
            block, block, lag_ssem.at[a, k], lag_rsem.at[a, k], "layer", ahead(layer, k, L)
        )

    def tile_copy(slot, k, source):
        held = pl.ds(source * RC, RC)
        if slot < LP:
            block = leaf_m.at[slot, held]
        elif slot < LP + A * T:
            block = cross_m.at[(slot - LP) // T, (slot - LP) % T, held]
        else:
            block = top_m.at[slot - LP - A * T, held]
        return remote(
            block, block, col_ssem.at[slot, k], col_rsem.at[slot, k], "col", ahead(col, k, C)
        )

    def tiles_arrive(slot):
        for k in range(1, C):
            tile_copy(slot, k, behind(col, k, C)).wait_recv()

    def send_tiles(slot):
        for k in range(1, C):
            tile_copy(slot, k, col).start()

    def each(start, stop, action):
        def body(index, carry):
            action(index)
            return carry

        loop(start, stop, body, 0)

    def mask(ref, lead, pattern, lead_pattern):
        def one(j):
            for i in range(SB):
                for n in range(SB):
                    bit = pattern[(*lead_pattern, i, j * SB + n)].astype(F32)
                    spread = jnp.full((W, W), bit, F32).astype(BF16)
                    at = (*lead, col * RC + j, pl.ds(i * W, W), pl.ds(n * W, W))
                    ref[at] = ref[at] * spread

        each(0, RC, one)

    def send_y(t, q):
        each(1, R, lambda k: y_copy(t, q, R - k, row).start())

    def turn_rhs(t):
        ld_rhs[t].wait()
        rhs_t[t] = rhs_in[t].T.reshape(Q, HQ, B)

    turn_rhs(0)
    ld_inv.wait()
    for q in range(Q):
        ybuf[0, q, row] = solve(inv, 0, rhs_t[0, q], False).astype(BF16)
    pl.semaphore_wait(barrier, (R - 1) + (L - 1) + (C - 1))
    for q in range(Q):
        send_y(0, q)
    for copy in ld_leaf:
        copy.wait()
    for slot in range(LP):
        mask(leaf_m, (slot,), leaf_pat, (0, slot))
        send_tiles(slot)
    for t in range(1, T):
        turn_rhs(t)
    for copy in ld_cross:
        copy.wait()
    for a in range(A):
        for t in range(T):
            mask(cross_m, (a, t), cross_pat, (0, a, t))
            send_tiles(LP + a * T + t)
    for copy in ld_top:
        copy.wait()
    for slot in range(AP):
        mask(top_m, (slot,), top_pat, (slot,))
        send_tiles(LP + A * T + slot)
    ld_arhs.wait()
    ld_ainv.wait()
    for a in range(A):
        arhs_t[a] = arhs_in[a].T.reshape(L, HL, B)

    def product(vectors, tiles, form=NT):
        return loop(
            1, R,
            lambda k, total: total + dot(vectors(k), tiles(k), form),
            dot(vectors(0), tiles(0), form),
        )

    arrived = set()

    def need(slot):
        if slot not in arrived:
            arrived.add(slot)
            tiles_arrive(slot)

    def whole(ref, lead, k):
        return ref[(lead, slice(None), k)].reshape(H, B)

    def fold_leaf(s):
        for t in range(s + 2, T):
            need(pair_index(t, s))
            term = product(lambda k: whole(ybuf, s, k), lambda k: leaf_m[pair_index(t, s), k])
            term = term.reshape(Q, HQ, B)
            fsum[t] = term if s == 0 else fsum[t] + term

    def fold_ancestor(s, a):
        need(LP + a * T + s)
        term = product(lambda k: whole(ybuf, s, k), lambda k: cross_m[a, s, k])
        term = term.reshape(L, HL, B)
        csum[a] = term if s == 0 else csum[a] + term

    for t in range(1, T):
        for q in range(Q):
            need(pair_index(t, t - 1))

            def arriving(k, total):
                source = row_from(k)
                y_copy(t - 1, q, k, source).wait_recv()
                return total + dot(ybuf[t - 1, q, source], leaf_m[pair_index(t, t - 1), source], NT)

            residual = rhs_t[t, q]
            if t > 1:
                residual = residual - fsum[t, q]
            own = dot(ybuf[t - 1, q, row], leaf_m[pair_index(t, t - 1), row], NT)
            residual = residual - loop(1, R, arriving, own)
            ybuf[t, q, row] = solve(inv, t, residual, False).astype(BF16)
            send_y(t, q)
        fold_leaf(t - 1)
        for a in range(A):
            fold_ancestor(t - 1, a)

    last = T - 1
    for q in range(Q):
        each(1, R, lambda k: y_copy(last, q, k, row_from(k)).wait_recv())
    for a in range(A):
        fold_ancestor(last, a)
        zs[a] = csum[a].astype(BF16)
        each(1, L, lambda k: lrs_copy(a, k).start())

    def layer_sum(a):
        def add_layer(k, total):
            lrs_copy(a, k).wait_recv()
            return total + zr[a, k].astype(F32)

        return loop(1, L, add_layer, csum[a, layer])

    for slot in range(AP):
        need(LP + A * T + slot)
    for a in range(A):
        residual = arhs_t[a, layer] - layer_sum(a)
        for s in range(a):
            if s == a - 1:
                each(1, R, lambda k: z_copy(s, k, row_from(k)).wait_recv())
            residual = residual - product(
                lambda k: zbuf[s, k], lambda k: top_m[pair_index(a, s), k]
            )
        zbuf[a, row] = solve(ainv, a, residual, False).astype(BF16)
        if a < A - 1:
            each(1, R, lambda k: z_copy(a, R - k, row).start())
    for a in range(A - 1, -1, -1):
        residual = zbuf[a, row].astype(F32)
        if a < A - 1:

            def partial(target):
                total = None
                for b in range(a + 1, A):
                    term = dot(xanc[b, layer], top_m[pair_index(b, a), target], NN)
                    total = term if total is None else total + term
                return total

            def send_part(k):
                asend[a, k] = partial(row_to(k)).astype(BF16)
                a_copy(a, k).start()

            each(1, R, lambda k: send_part(R - k))

            def add_part(k, total):
                a_copy(a, k).wait_recv()
                return total + arecv[a, k].astype(F32)

            residual = residual - loop(1, R, add_part, partial(row))
        xanc[a, layer] = solve(ainv, a, residual, True).astype(BF16)
        each(1, L, lambda k: lag_copy(a, k, layer).start())

    def out_place(slot, owner):
        cols = pl.ds(pl.multiple_of(owner * H, H), H)
        return leaf_out.at[0, slot, :, cols] if slot < T else anc_out.at[slot - T, :, cols]

    def out_copy(slot, k, source):
        block = out_place(slot, source)
        return remote(
            block, block, out_ssem.at[slot, k], out_rsem.at[slot, k], "col", ahead(col, k, C)
        )

    def emit(slot, value):
        turned = value.astype(F32).T.astype(BF16)
        if slot < T:
            leaf_out[0, slot, :, my_cols] = turned
        else:
            anc_out[slot - T, :, my_cols] = turned
        for k in range(1, C):
            out_copy(slot, k, col).start()

    def anc_chunk(a, q):
        return xanc[a, pl.ds(q * LQ, LQ)].reshape(HQ, B)

    def fold_back(t, vector, tiles, first=False):
        def one(k):
            term = dot(vector, tiles(k), NN).reshape(Q, HQ, B)
            bsum[t, :, k] = term if first else bsum[t, :, k] + term

        each(0, R, one)

    def fold_cross(a, t):
        fold_back(t, xanc[a].reshape(H, B), lambda k: cross_m[a, t, k], a == A - 1)

    def start_level(t, q):
        def value(target):
            total = bsum[t, q, target]
            if t == T - 1:
                return total + dot(anc_chunk(0, q), cross_m[0, t, target], NN)
            return total + dot(xbuf[t + 1, q], leaf_m[pair_index(t + 1, t), target], NN)

        def send_part(k):
            bsend[t, q, k] = value(row_to(k)).astype(BF16)
            b_copy(t, q, k).start()

        each(1, R, lambda k: send_part(R - k))
        bown[t, q] = value(row)

    for a in range(A - 1, 0, -1):
        each(1, L, lambda k: lag_copy(a, k, behind(layer, k, L)).wait_recv())
        fold_cross(a, T - 1)
    each(1, L, lambda k: lag_copy(0, k, behind(layer, k, L)).wait_recv())
    for q in range(Q):
        start_level(T - 1, q)
    for t in range(T - 2, -1, -1):
        for a in range(A - 1, -1, -1):
            fold_cross(a, t)
    for a in range(A):
        emit(T + a, xanc[a].reshape(H, B))
    for t in range(T - 1, -1, -1):
        for q in range(Q):

            def add_part(k, total):
                b_copy(t, q, k).wait_recv()
                return total + brecv[t, q, k].astype(F32)

            residual = ybuf[t, q, row].astype(F32) - loop(1, R, add_part, bown[t, q])
            xbuf[t, q] = solve(inv, t, residual, True).astype(BF16)
            if t > 0:
                start_level(t - 1, q)
        emit(t, xbuf[t].reshape(H, B))
        for lower in range(t - 1):
            fold_back(lower, xbuf[t].reshape(H, B), lambda k: leaf_m[pair_index(t, lower), k])

    for slot in range(LP + A * T + AP):
        for k in range(1, C):
            tile_copy(slot, k, col).wait_send()
    for t in range(T):
        for q in range(Q):
            each(1, R, lambda k: y_copy(t, q, k, row).wait_send())
            each(1, R, lambda k: b_copy(t, q, k).wait_send())
    for a in range(A - 1):
        each(1, R, lambda k: z_copy(a, k, row).wait_send())
        each(1, R, lambda k: a_copy(a, k).wait_send())
    for a in range(A):
        each(1, L, lambda k: lrs_copy(a, k).wait_send())
        each(1, L, lambda k: lag_copy(a, k, layer).wait_send())
    for slot in range(T + A):
        for k in range(1, C):
            out_copy(slot, k, col).wait_send()
            out_copy(slot, k, behind(col, k, C)).wait_recv()


def local(R, L, C, *arrays):
    leaf_rhs, anc_rhs = arrays[:2]
    T = leaf_rhs.shape[1]
    A = anc_rhs.shape[0]
    B = leaf_rhs.shape[2]
    H = leaf_rhs.shape[3] // C
    W = arrays[8].shape[-1]
    Q = 2 if R <= 4 and L % 2 == 0 else 1
    HQ, HL = H // Q, H // L
    SB = B // W
    LP, AP = T * (T - 1) // 2, A * (A - 1) // 2
    dims = (R, L, C, Q, T, A, B, H, HQ, HL, W)
    vmem = pltpu.VMEM
    dma = pltpu.SemaphoreType.DMA
    slots = LP + A * T + AP
    scratch = [
        vmem((T, B, H), F32), vmem((A, B, H), F32),
        vmem((T, SB, W, W), BF16), vmem((A, SB, W, W), BF16),
        vmem((T, Q, HQ, B), F32), vmem((A, L, HL, B), F32),
        vmem((LP, R, B, B), BF16), vmem((A, T, R, B, B), BF16), vmem((AP, R, B, B), BF16),
        vmem((T, Q, R, HQ, B), BF16), vmem((T, Q, HQ, B), F32), vmem((A, L, HL, B), F32),
        vmem((A, L, HL, B), BF16), vmem((A, L, HL, B), BF16),
        vmem((A, R, HL, B), BF16), vmem((A, L, HL, B), BF16),
        vmem((A, R, HL, B), BF16), vmem((A, R, HL, B), BF16),
        vmem((T, Q, R, HQ, B), F32), vmem((T, Q, HQ, B), F32),
        vmem((T, Q, R, HQ, B), BF16), vmem((T, Q, R, HQ, B), BF16),
        vmem((T, Q, HQ, B), BF16),
        dma((T + 3 + 3 * (R // C),)),
        dma((slots, C)), dma((slots, C)),
        dma((T, Q, R)), dma((T, Q, R)), dma((A, R)), dma((A, R)),
        dma((A, L)), dma((A, L)), dma((A, L)), dma((A, L)),
        dma((A, R)), dma((A, R)), dma((T, Q, R)), dma((T, Q, R)),
        dma((T + A, C)), dma((T + A, C)),
    ]
    anywhere = pl.BlockSpec(memory_space=pl.ANY)
    scalars = pl.BlockSpec(memory_space=pltpu.SMEM)
    return pl.pallas_call(
        functools.partial(kernel, dims),
        out_shape=(
            vmem(leaf_rhs.shape, BF16),
            vmem(anc_rhs.shape, BF16),
        ),
        in_specs=[anywhere] * 5 + [scalars] * 3 + [anywhere] * 2,
        out_specs=(pl.BlockSpec(memory_space=vmem),) * 2,
        scratch_shapes=scratch,
        compiler_params=pltpu.CompilerParams(
            collective_id=0, has_side_effects=True, vmem_limit_bytes=56 * 1024 * 1024
        ),
    )(*arrays)


def solution(mesh):
    in_specs = (
        P("layer", None, "row", None),
        P(None, "row", None),
        P("layer", None, "row", "col"),
        P("layer", None, None, "row", "col"),
        P(None, "row", "col"),
        P("layer", None, "row", "col"),
        P("layer", None, None, "row", "col"),
        P(None, "row", "col"),
        P("layer", None, None, None, None),
        P(),
    )
    out_specs = (P("layer", None, "row", None), P(None, "row", None))
    sizes = mesh.shape
    return jax.shard_map(
        functools.partial(local, sizes["row"], sizes["layer"], sizes["col"]),
        mesh=mesh, in_specs=in_specs, out_specs=out_specs, check_vma=False,
    )
```

```python
import functools

import jax
import jax.numpy as jnp
from jax import lax
from jax.experimental import pallas as pl
from jax.experimental.pallas import tpu as pltpu
from jax.sharding import PartitionSpec as P

MESH = pl.DeviceIdType.MESH
NT = (((1,), (1,)), ((), ()))
NN = (((1,), (0,)), ((), ()))
F32 = jnp.float32
BF16 = jnp.bfloat16


def pair_index(target, source):
    return target * (target - 1) // 2 + source


def dot(left, right, form):
    return lax.dot_general(left, right, form, preferred_element_type=F32)


def loop(start, stop, body, init):
    if stop - start <= 4:
        carry = init
        for index in range(start, stop):
            carry = body(index, carry)
        return carry
    return lax.fori_loop(start, stop, body, init)


def solve(inverse, level, residual, flipped):
    wide = inverse.shape[-1]
    pieces = []
    rounded = residual.astype(BF16)
    for block in range(inverse.shape[1]):
        part = rounded[:, block * wide : (block + 1) * wide]
        pieces.append(dot(part, inverse[level, block], NN if flipped else NT))
    return jnp.concatenate(pieces, axis=1)


def kernel(
    dims,
    leaf_rhs, anc_rhs, leaf_tiles, cross_tiles, top_tiles,
    leaf_pat, cross_pat, top_pat, leaf_inv, anc_inv,
    leaf_out, anc_out,
    rhs_in, arhs_in, inv, ainv, rhs_t, arhs_t, leaf_m, cross_m, top_m,
    ybuf, fsum, csum, zs, zr, zbuf, xanc, asend, arecv,
    bsum, bown, bsend, brecv, xbuf,
    load_sem, col_ssem, col_rsem, y_ssem, y_rsem, z_ssem, z_rsem,
    lrs_ssem, lrs_rsem, lag_ssem, lag_rsem, a_ssem, a_rsem, b_ssem, b_rsem,
    out_ssem, out_rsem,
):
    R, L, C, Q, T, A, B, H, HQ, HL, W = dims
    RC = R // C
    LQ = L // Q
    SB = B // W
    LP = T * (T - 1) // 2
    AP = A * (A - 1) // 2
    row = lax.axis_index("row")
    layer = lax.axis_index("layer")
    col = lax.axis_index("col")

    def ahead(axis_index, step, size):
        return lax.rem(axis_index + step, size)

    def behind(axis_index, step, size):
        return lax.rem(axis_index + size - step, size)

    binary = R & (R - 1) == 0

    def row_to(step):
        if not binary:
            return ahead(row, step, R)
        total, place = 0, 1
        while place < R:
            total = total + lax.rem(lax.div(row, place) + step // place, 2) * place
            place *= 2
        return total

    def row_from(step):
        return row_to(step) if binary else behind(row, step, R)

    loads = []

    def load(src, dst):
        copy = pltpu.make_async_copy(src, dst, load_sem.at[len(loads)])
        copy.start()
        loads.append(copy)
        return copy

    my_cols = pl.ds(pl.multiple_of(col * H, H), H)
    ld_rhs = [load(leaf_rhs.at[0, 0, :, my_cols], rhs_in.at[0])]
    ld_inv = load(leaf_inv.at[0, :, pl.ds(row * SB, SB)], inv)
    ld_leaf = [
        load(leaf_tiles.at[0, :, :, pl.ds(j * B, B)], leaf_m.at[:, col * RC + j])
        for j in range(RC)
    ]
    for t in range(1, T):
        ld_rhs.append(load(leaf_rhs.at[0, t, :, my_cols], rhs_in.at[t]))
    ld_cross = [
        load(cross_tiles.at[0, :, :, :, pl.ds(j * B, B)], cross_m.at[:, :, col * RC + j])
        for j in range(RC)
    ]
    ld_top = [
        load(top_tiles.at[:, :, pl.ds(j * B, B)], top_m.at[:, col * RC + j])
        for j in range(RC)
    ]
    ld_arhs = load(anc_rhs.at[:, :, my_cols], arhs_in)
    ld_ainv = load(anc_inv.at[:, pl.ds(row * SB, SB)], ainv)

    barrier = pltpu.get_barrier_semaphore()
    for name, mine, size in (("row", row, R), ("layer", layer, L), ("col", col, C)):
        for step in range(1, size):
            pl.semaphore_signal(
                barrier, inc=1, device_id={name: ahead(mine, step, size)}, device_id_type=MESH
            )

    def remote(src, dst, ssem, rsem, name, target):
        return pltpu.make_async_remote_copy(
            src_ref=src, dst_ref=dst, send_sem=ssem, recv_sem=rsem,
            device_id={name: target}, device_id_type=MESH,
        )

    def y_copy(t, q, k, source):
        block = ybuf.at[t, q, source]
        return remote(block, block, y_ssem.at[t, q, k], y_rsem.at[t, q, k], "row", row_to(k))

    def z_copy(a, k, source):
        block = zbuf.at[a, source]
        return remote(block, block, z_ssem.at[a, k], z_rsem.at[a, k], "row", row_to(k))

    def a_copy(a, k):
        return remote(
            asend.at[a, k], arecv.at[a, k], a_ssem.at[a, k], a_rsem.at[a, k], "row", row_to(k)
        )

    def b_copy(t, q, k):
        return remote(
            bsend.at[t, q, k], brecv.at[t, q, k], b_ssem.at[t, q, k], b_rsem.at[t, q, k],
            "row", row_to(k),
        )

    def lrs_copy(a, k):
        target = ahead(layer, k, L)
        return remote(
            zs.at[a, target], zr.at[a, k], lrs_ssem.at[a, k], lrs_rsem.at[a, k], "layer", target
        )

    def lag_copy(a, k, source):
        block = xanc.at[a, source]
        return remote(
            block, block, lag_ssem.at[a, k], lag_rsem.at[a, k], "layer", ahead(layer, k, L)
        )

    def tile_copy(slot, k, source):
        held = pl.ds(source * RC, RC)
        if slot < LP:
            block = leaf_m.at[slot, held]
        elif slot < LP + A * T:
            block = cross_m.at[(slot - LP) // T, (slot - LP) % T, held]
        else:
            block = top_m.at[slot - LP - A * T, held]
        return remote(
            block, block, col_ssem.at[slot, k], col_rsem.at[slot, k], "col", ahead(col, k, C)
        )

    def tiles_arrive(slot):
        for k in range(1, C):
            tile_copy(slot, k, behind(col, k, C)).wait_recv()

    def send_tiles(slot):
        for k in range(1, C):
            tile_copy(slot, k, col).start()

    def each(start, stop, action):
        def body(index, carry):
            action(index)
            return carry

        loop(start, stop, body, 0)

    def mask(ref, lead, pattern, lead_pattern):
        def one(j):
            for i in range(SB):
                for n in range(SB):
                    bit = pattern[(*lead_pattern, i, j * SB + n)].astype(F32)
                    spread = jnp.full((W, W), bit, F32).astype(BF16)
                    at = (*lead, col * RC + j, pl.ds(i * W, W), pl.ds(n * W, W))
                    ref[at] = ref[at] * spread

        each(0, RC, one)

    def send_y(t, q):
        each(1, R, lambda k: y_copy(t, q, R - k, row).start())

    def turn_rhs(t):
        ld_rhs[t].wait()
        rhs_t[t] = rhs_in[t].T.reshape(Q, HQ, B)

    turn_rhs(0)
    ld_inv.wait()
    for q in range(Q):
        ybuf[0, q, row] = solve(inv, 0, rhs_t[0, q], False).astype(BF16)
    pl.semaphore_wait(barrier, (R - 1) + (L - 1) + (C - 1))
    for q in range(Q):
        send_y(0, q)
    for copy in ld_leaf:
        copy.wait()
    for slot in range(LP):
        mask(leaf_m, (slot,), leaf_pat, (0, slot))
        send_tiles(slot)
    for t in range(1, T):
        turn_rhs(t)
    def prepare_cross():
        for copy in ld_cross:
            copy.wait()
        for t in range(T):
            for a in range(A):
                mask(cross_m, (a, t), cross_pat, (0, a, t))
                send_tiles(LP + a * T + t)

    def prepare_top():
        for copy in ld_top:
            copy.wait()
        for slot in range(AP):
            mask(top_m, (slot,), top_pat, (slot,))
            send_tiles(LP + A * T + slot)
        ld_arhs.wait()
        ld_ainv.wait()
        for a in range(A):
            arhs_t[a] = arhs_in[a].T.reshape(L, HL, B)

    def product(vectors, tiles, form=NT):
        return loop(
            1, R,
            lambda k, total: total + dot(vectors(k), tiles(k), form),
            dot(vectors(0), tiles(0), form),
        )

    arrived = set()

    def need(slot):
        if slot not in arrived:
            arrived.add(slot)
            tiles_arrive(slot)

    def whole(ref, lead, k):
        return ref[(lead, slice(None), k)].reshape(H, B)

    def fold_leaf(s):
        for t in range(s + 2, T):
            need(pair_index(t, s))
            term = product(lambda k: whole(ybuf, s, k), lambda k: leaf_m[pair_index(t, s), k])
            term = term.reshape(Q, HQ, B)
            fsum[t] = term if s == 0 else fsum[t] + term

    def fold_ancestor(s, a):
        need(LP + a * T + s)
        term = product(lambda k: whole(ybuf, s, k), lambda k: cross_m[a, s, k])
        term = term.reshape(L, HL, B)
        csum[a] = term if s == 0 else csum[a] + term

    for t in range(1, T):
        for q in range(Q):
            need(pair_index(t, t - 1))

            def arriving(k, total):
                source = row_from(k)
                y_copy(t - 1, q, k, source).wait_recv()
                return total + dot(ybuf[t - 1, q, source], leaf_m[pair_index(t, t - 1), source], NT)

            residual = rhs_t[t, q]
            if t > 1:
                residual = residual - fsum[t, q]
            own = dot(ybuf[t - 1, q, row], leaf_m[pair_index(t, t - 1), row], NT)
            residual = residual - loop(1, R, arriving, own)
            ybuf[t, q, row] = solve(inv, t, residual, False).astype(BF16)
            send_y(t, q)
        fold_leaf(t - 1)
        if t == 1:
            prepare_cross()
        if t == T - 1:
            prepare_top()
            for s in range(t):
                for a in range(A):
                    fold_ancestor(s, a)

    last = T - 1
    for a in range(A):
        need(LP + a * T + last)

    def last_block(source, a):
        term = dot(whole(ybuf, last, source), cross_m[a, last, source], NT)
        csum[a] += term.reshape(L, HL, B)

    for a in range(A):
        last_block(row, a)

    def last_arrival(k):
        for q in range(Q):
            y_copy(last, q, k, row_from(k)).wait_recv()
        for a in range(A):
            last_block(row_from(k), a)

    each(1, R - 1, last_arrival)
    for q in range(Q):
        y_copy(last, q, R - 1, row_from(R - 1)).wait_recv()
    for a in range(A):
        last_block(row_from(R - 1), a)
        zs[a] = csum[a].astype(BF16)
        each(1, L, lambda k: lrs_copy(a, k).start())

    def layer_sum(a):
        def add_layer(k, total):
            lrs_copy(a, k).wait_recv()
            return total + zr[a, k].astype(F32)

        return loop(1, L, add_layer, csum[a, layer])

    for slot in range(AP):
        need(LP + A * T + slot)
    for a in range(A):
        residual = arhs_t[a, layer] - layer_sum(a)
        for s in range(a):

            def add_block(k, total):
                source = row_from(k)
                if s == a - 1:
                    z_copy(s, k, source).wait_recv()
                return total - dot(zbuf[s, source], top_m[pair_index(a, s), source], NT)

            residual = residual - dot(zbuf[s, row], top_m[pair_index(a, s), row], NT)
            residual = loop(1, R, add_block, residual)
        zbuf[a, row] = solve(ainv, a, residual, False).astype(BF16)
        if a < A - 1:
            each(1, R, lambda k: z_copy(a, R - k, row).start())
    for a in range(A - 1, -1, -1):
        residual = zbuf[a, row].astype(F32)
        if a < A - 1:

            def partial(target):
                total = None
                for b in range(a + 1, A):
                    term = dot(xanc[b, layer], top_m[pair_index(b, a), target], NN)
                    total = term if total is None else total + term
                return total

            def send_part(k):
                asend[a, k] = partial(row_to(k)).astype(BF16)
                a_copy(a, k).start()

            each(1, R, lambda k: send_part(R - k))

            def add_part(k, total):
                a_copy(a, k).wait_recv()
                return total + arecv[a, k].astype(F32)

            residual = residual - loop(1, R, add_part, partial(row))
        xanc[a, layer] = solve(ainv, a, residual, True).astype(BF16)
        each(1, L, lambda k: lag_copy(a, k, layer).start())

    def out_place(slot, owner):
        cols = pl.ds(pl.multiple_of(owner * H, H), H)
        return leaf_out.at[0, slot, :, cols] if slot < T else anc_out.at[slot - T, :, cols]

    def out_copy(slot, k, source):
        block = out_place(slot, source)
        return remote(
            block, block, out_ssem.at[slot, k], out_rsem.at[slot, k], "col", ahead(col, k, C)
        )

    def emit(slot, value):
        turned = value.astype(F32).T.astype(BF16)
        if slot < T:
            leaf_out[0, slot, :, my_cols] = turned
        else:
            anc_out[slot - T, :, my_cols] = turned
        for k in range(1, C):
            out_copy(slot, k, col).start()

    def anc_chunk(a, q):
        return xanc[a, pl.ds(q * LQ, LQ)].reshape(HQ, B)

    def fold_back(t, vector, tiles, first=False):
        def one(k):
            term = dot(vector, tiles(k), NN).reshape(Q, HQ, B)
            bsum[t, :, k] = term if first else bsum[t, :, k] + term

        each(0, R, one)

    def fold_cross(a, t):
        fold_back(t, xanc[a].reshape(H, B), lambda k: cross_m[a, t, k], a == A - 1)

    def start_level(t, q):
        def value(target):
            total = bsum[t, q, target]
            if t == T - 1:
                return total + dot(anc_chunk(0, q), cross_m[0, t, target], NN)
            return total + dot(xbuf[t + 1, q], leaf_m[pair_index(t + 1, t), target], NN)

        def send_part(k):
            bsend[t, q, k] = value(row_to(k)).astype(BF16)
            b_copy(t, q, k).start()

        each(1, R, lambda k: send_part(R - k))
        bown[t, q] = value(row)

    for a in range(A - 1, 0, -1):
        each(1, L, lambda k: lag_copy(a, k, behind(layer, k, L)).wait_recv())
        fold_cross(a, T - 1)
    each(1, L, lambda k: lag_copy(0, k, behind(layer, k, L)).wait_recv())
    for q in range(Q):
        start_level(T - 1, q)
    for t in range(T - 2, -1, -1):
        for a in range(A - 1, -1, -1):
            fold_cross(a, t)
    for a in range(A):
        emit(T + a, xanc[a].reshape(H, B))
    for t in range(T - 1, -1, -1):
        for q in range(Q):

            def add_part(k, total):
                b_copy(t, q, k).wait_recv()
                return total + brecv[t, q, k].astype(F32)

            residual = ybuf[t, q, row].astype(F32) - loop(1, R, add_part, bown[t, q])
            xbuf[t, q] = solve(inv, t, residual, True).astype(BF16)
            if t > 0:
                start_level(t - 1, q)
        emit(t, xbuf[t].reshape(H, B))
        for lower in range(t - 1):
            fold_back(lower, xbuf[t].reshape(H, B), lambda k: leaf_m[pair_index(t, lower), k])

    for slot in range(LP + A * T + AP):
        for k in range(1, C):
            tile_copy(slot, k, col).wait_send()
    for t in range(T):
        for q in range(Q):
            each(1, R, lambda k: y_copy(t, q, k, row).wait_send())
            each(1, R, lambda k: b_copy(t, q, k).wait_send())
    for a in range(A - 1):
        each(1, R, lambda k: z_copy(a, k, row).wait_send())
        each(1, R, lambda k: a_copy(a, k).wait_send())
    for a in range(A):
        each(1, L, lambda k: lrs_copy(a, k).wait_send())
        each(1, L, lambda k: lag_copy(a, k, layer).wait_send())
    for slot in range(T + A):
        for k in range(1, C):
            out_copy(slot, k, col).wait_send()
            out_copy(slot, k, behind(col, k, C)).wait_recv()


def local(R, L, C, *arrays):
    leaf_rhs, anc_rhs = arrays[:2]
    T = leaf_rhs.shape[1]
    A = anc_rhs.shape[0]
    B = leaf_rhs.shape[2]
    H = leaf_rhs.shape[3] // C
    W = arrays[8].shape[-1]
    Q = 2 if R <= 4 and L % 2 == 0 else 1
    HQ, HL = H // Q, H // L
    SB = B // W
    LP, AP = T * (T - 1) // 2, A * (A - 1) // 2
    dims = (R, L, C, Q, T, A, B, H, HQ, HL, W)
    vmem = pltpu.VMEM
    dma = pltpu.SemaphoreType.DMA
    slots = LP + A * T + AP
    scratch = [
        vmem((T, B, H), F32), vmem((A, B, H), F32),
        vmem((T, SB, W, W), BF16), vmem((A, SB, W, W), BF16),
        vmem((T, Q, HQ, B), F32), vmem((A, L, HL, B), F32),
        vmem((LP, R, B, B), BF16), vmem((A, T, R, B, B), BF16), vmem((AP, R, B, B), BF16),
        vmem((T, Q, R, HQ, B), BF16), vmem((T, Q, HQ, B), F32), vmem((A, L, HL, B), F32),
        vmem((A, L, HL, B), BF16), vmem((A, L, HL, B), BF16),
        vmem((A, R, HL, B), BF16), vmem((A, L, HL, B), BF16),
        vmem((A, R, HL, B), BF16), vmem((A, R, HL, B), BF16),
        vmem((T, Q, R, HQ, B), F32), vmem((T, Q, HQ, B), F32),
        vmem((T, Q, R, HQ, B), BF16), vmem((T, Q, R, HQ, B), BF16),
        vmem((T, Q, HQ, B), BF16),
        dma((T + 3 + 3 * (R // C),)),
        dma((slots, C)), dma((slots, C)),
        dma((T, Q, R)), dma((T, Q, R)), dma((A, R)), dma((A, R)),
        dma((A, L)), dma((A, L)), dma((A, L)), dma((A, L)),
        dma((A, R)), dma((A, R)), dma((T, Q, R)), dma((T, Q, R)),
        dma((T + A, C)), dma((T + A, C)),
    ]
    anywhere = pl.BlockSpec(memory_space=pl.ANY)
    scalars = pl.BlockSpec(memory_space=pltpu.SMEM)
    return pl.pallas_call(
        functools.partial(kernel, dims),
        out_shape=(
            vmem(leaf_rhs.shape, BF16),
            vmem(anc_rhs.shape, BF16),
        ),
        in_specs=[anywhere] * 5 + [scalars] * 3 + [anywhere] * 2,
        out_specs=(pl.BlockSpec(memory_space=vmem),) * 2,
        scratch_shapes=scratch,
        compiler_params=pltpu.CompilerParams(
            collective_id=0, has_side_effects=True, vmem_limit_bytes=56 * 1024 * 1024
        ),
    )(*arrays)


def solution(mesh):
    in_specs = (
        P("layer", None, "row", None),
        P(None, "row", None),
        P("layer", None, "row", "col"),
        P("layer", None, None, "row", "col"),
        P(None, "row", "col"),
        P("layer", None, "row", "col"),
        P("layer", None, None, "row", "col"),
        P(None, "row", "col"),
        P("layer", None, None, None, None),
        P(),
    )
    out_specs = (P("layer", None, "row", None), P(None, "row", None))
    sizes = mesh.shape
    return jax.shard_map(
        functools.partial(local, sizes["row"], sizes["layer"], sizes["col"]),
        mesh=mesh, in_specs=in_specs, out_specs=out_specs, check_vma=False,
    )
```

```python
import functools

import jax
import jax.numpy as jnp
from jax import lax
from jax.experimental import pallas as pl
from jax.experimental.pallas import tpu as pltpu
from jax.sharding import PartitionSpec as P

MESH = pl.DeviceIdType.MESH
NT = (((1,), (1,)), ((), ()))
NN = (((1,), (0,)), ((), ()))
F32 = jnp.float32
BF16 = jnp.bfloat16


def pair_index(target, source):
    return target * (target - 1) // 2 + source


def dot(left, right, form):
    return lax.dot_general(left, right, form, preferred_element_type=F32)


def loop(start, stop, body, init):
    if stop - start <= 4:
        carry = init
        for index in range(start, stop):
            carry = body(index, carry)
        return carry
    return lax.fori_loop(start, stop, body, init)


def solve(inverse, level, residual, flipped):
    wide = inverse.shape[-1]
    pieces = []
    rounded = residual.astype(BF16)
    for block in range(inverse.shape[1]):
        part = rounded[:, block * wide : (block + 1) * wide]
        pieces.append(dot(part, inverse[level, block], NN if flipped else NT))
    return jnp.concatenate(pieces, axis=1)


def kernel(
    dims,
    leaf_rhs, anc_rhs, leaf_tiles, cross_tiles, top_tiles,
    leaf_pat, cross_pat, top_pat, leaf_inv, anc_inv,
    leaf_out, anc_out,
    rhs_in, arhs_in, inv, ainv, rhs_t, arhs_t, leaf_m, cross_m, top_m,
    ybuf, fsum, csum, zs, zr, zbuf, xanc, asend, arecv,
    bsum, bown, bsend, brecv, xbuf,
    load_sem, col_ssem, col_rsem, y_ssem, y_rsem, z_ssem, z_rsem,
    lrs_ssem, lrs_rsem, lag_ssem, lag_rsem, a_ssem, a_rsem, b_ssem, b_rsem,
    out_ssem, out_rsem,
):
    R, L, C, Q, T, A, B, H, HQ, HL, W = dims
    RC = R // C
    LQ = L // Q
    SB = B // W
    LP = T * (T - 1) // 2
    AP = A * (A - 1) // 2
    row = lax.axis_index("row")
    layer = lax.axis_index("layer")
    col = lax.axis_index("col")

    def ahead(axis_index, step, size):
        return lax.rem(axis_index + step, size)

    def behind(axis_index, step, size):
        return lax.rem(axis_index + size - step, size)

    binary = R & (R - 1) == 0

    def row_to(step):
        if not binary:
            return ahead(row, step, R)
        total, place = 0, 1
        while place < R:
            total = total + lax.rem(lax.div(row, place) + step // place, 2) * place
            place *= 2
        return total

    def row_from(step):
        return row_to(step) if binary else behind(row, step, R)

    loads = []

    def load(src, dst):
        copy = pltpu.make_async_copy(src, dst, load_sem.at[len(loads)])
        copy.start()
        loads.append(copy)
        return copy

    my_cols = pl.ds(pl.multiple_of(col * H, H), H)
    ld_rhs = [load(leaf_rhs.at[0, 0, :, my_cols], rhs_in.at[0])]
    ld_inv = load(leaf_inv.at[0, :, pl.ds(row * SB, SB)], inv)
    ld_leaf = [
        load(leaf_tiles.at[0, :, :, pl.ds(j * B, B)], leaf_m.at[:, col * RC + j])
        for j in range(RC)
    ]
    for t in range(1, T):
        ld_rhs.append(load(leaf_rhs.at[0, t, :, my_cols], rhs_in.at[t]))
    ld_cross = [
        load(cross_tiles.at[0, :, :, :, pl.ds(j * B, B)], cross_m.at[:, :, col * RC + j])
        for j in range(RC)
    ]
    ld_top = [
        load(top_tiles.at[:, :, pl.ds(j * B, B)], top_m.at[:, col * RC + j])
        for j in range(RC)
    ]
    ld_arhs = load(anc_rhs.at[:, :, my_cols], arhs_in)
    ld_ainv = load(anc_inv.at[:, pl.ds(row * SB, SB)], ainv)

    barrier = pltpu.get_barrier_semaphore()
    for name, mine, size in (("row", row, R), ("layer", layer, L), ("col", col, C)):
        for step in range(1, size):
            pl.semaphore_signal(
                barrier, inc=1, device_id={name: ahead(mine, step, size)}, device_id_type=MESH
            )

    def remote(src, dst, ssem, rsem, name, target):
        return pltpu.make_async_remote_copy(
            src_ref=src, dst_ref=dst, send_sem=ssem, recv_sem=rsem,
            device_id={name: target}, device_id_type=MESH,
        )

    def y_copy(t, q, k, source):
        block = ybuf.at[t, q, source]
        return remote(block, block, y_ssem.at[t, q, k], y_rsem.at[t, q, k], "row", row_to(k))

    def z_copy(a, k, source):
        block = zbuf.at[a, source]
        return remote(block, block, z_ssem.at[a, k], z_rsem.at[a, k], "row", row_to(k))

    def a_copy(a, k):
        return remote(
            asend.at[a, k], arecv.at[a, k], a_ssem.at[a, k], a_rsem.at[a, k], "row", row_to(k)
        )

    def b_copy(t, q, k):
        return remote(
            bsend.at[t, q, k], brecv.at[t, q, k], b_ssem.at[t, q, k], b_rsem.at[t, q, k],
            "row", row_to(k),
        )

    def lrs_copy(a, k):
        target = ahead(layer, k, L)
        return remote(
            zs.at[a, target], zr.at[a, k], lrs_ssem.at[a, k], lrs_rsem.at[a, k], "layer", target
        )

    def lag_copy(a, k, source):
        block = xanc.at[a, source]
        return remote(
            block, block, lag_ssem.at[a, k], lag_rsem.at[a, k], "layer", ahead(layer, k, L)
        )

    def tile_copy(slot, k, source):
        held = pl.ds(source * RC, RC)
        if slot < LP:
            block = leaf_m.at[slot, held]
        elif slot < LP + A * T:
            block = cross_m.at[(slot - LP) // T, (slot - LP) % T, held]
        else:
            block = top_m.at[slot - LP - A * T, held]
        return remote(
            block, block, col_ssem.at[slot, k], col_rsem.at[slot, k], "col", ahead(col, k, C)
        )

    def tiles_arrive(slot):
        for k in range(1, C):
            tile_copy(slot, k, behind(col, k, C)).wait_recv()

    def send_tiles(slot):
        for k in range(1, C):
            tile_copy(slot, k, col).start()

    def each(start, stop, action):
        def body(index, carry):
            action(index)
            return carry

        loop(start, stop, body, 0)

    def mask(ref, lead, pattern, lead_pattern):
        def one(j):
            for i in range(SB):
                for n in range(SB):
                    bit = pattern[(*lead_pattern, i, j * SB + n)].astype(F32)
                    spread = jnp.full((W, W), bit, F32).astype(BF16)
                    at = (*lead, col * RC + j, pl.ds(i * W, W), pl.ds(n * W, W))
                    ref[at] = ref[at] * spread

        each(0, RC, one)

    def send_y(t, q):
        each(1, R, lambda k: y_copy(t, q, R - k, row).start())

    def turn_rhs(t):
        ld_rhs[t].wait()
        rhs_t[t] = rhs_in[t].T.reshape(Q, HQ, B)

    turn_rhs(0)
    ld_inv.wait()
    for q in range(Q):
        ybuf[0, q, row] = solve(inv, 0, rhs_t[0, q], False).astype(BF16)
    pl.semaphore_wait(barrier, (R - 1) + (L - 1) + (C - 1))
    for q in range(Q):
        send_y(0, q)
    for copy in ld_leaf:
        copy.wait()
    for slot in range(LP):
        mask(leaf_m, (slot,), leaf_pat, (0, slot))
        send_tiles(slot)
    for t in range(1, T):
        turn_rhs(t)
    def prepare_cross():
        for copy in ld_cross:
            copy.wait()
        for t in range(T):
            for a in range(A):
                mask(cross_m, (a, t), cross_pat, (0, a, t))
                send_tiles(LP + a * T + t)

    def prepare_top():
        for copy in ld_top:
            copy.wait()
        for slot in range(AP):
            mask(top_m, (slot,), top_pat, (slot,))
            send_tiles(LP + A * T + slot)
        ld_arhs.wait()
        ld_ainv.wait()
        for a in range(A):
            arhs_t[a] = arhs_in[a].T.reshape(L, HL, B)

    def product(vectors, tiles, form=NT):
        return loop(
            1, R,
            lambda k, total: total + dot(vectors(k), tiles(k), form),
            dot(vectors(0), tiles(0), form),
        )

    arrived = set()

    def need(slot):
        if slot not in arrived:
            arrived.add(slot)
            tiles_arrive(slot)

    def whole(ref, lead, k):
        return ref[(lead, slice(None), k)].reshape(H, B)

    def fold_leaf(s):
        for t in range(s + 2, T):
            need(pair_index(t, s))
            term = product(lambda k: whole(ybuf, s, k), lambda k: leaf_m[pair_index(t, s), k])
            term = term.reshape(Q, HQ, B)
            fsum[t] = term if s == 0 else fsum[t] + term

    def fold_ancestor(s, a):
        need(LP + a * T + s)
        term = product(lambda k: whole(ybuf, s, k), lambda k: cross_m[a, s, k])
        term = term.reshape(L, HL, B)
        csum[a] = term if s == 0 else csum[a] + term

    for t in range(1, T):
        for q in range(Q):
            need(pair_index(t, t - 1))

            def arriving(k, total):
                source = row_from(k)
                y_copy(t - 1, q, k, source).wait_recv()
                return total + dot(ybuf[t - 1, q, source], leaf_m[pair_index(t, t - 1), source], NT)

            residual = rhs_t[t, q]
            if t > 1:
                residual = residual - fsum[t, q]
            own = dot(ybuf[t - 1, q, row], leaf_m[pair_index(t, t - 1), row], NT)
            residual = residual - loop(1, R, arriving, own)
            ybuf[t, q, row] = solve(inv, t, residual, False).astype(BF16)
            send_y(t, q)
        fold_leaf(t - 1)
        if t == 1:
            prepare_cross()
        if t == T - 1:
            prepare_top()
            for s in range(t):
                for a in range(A):
                    fold_ancestor(s, a)

    last = T - 1
    for a in range(A):
        need(LP + a * T + last)

    def last_block(source, a):
        term = dot(whole(ybuf, last, source), cross_m[a, last, source], NT)
        csum[a] += term.reshape(L, HL, B)

    for a in range(A):
        last_block(row, a)

    def last_arrival(k):
        for q in range(Q):
            y_copy(last, q, k, row_from(k)).wait_recv()
        for a in range(A):
            last_block(row_from(k), a)

    each(1, R - 1, last_arrival)
    for q in range(Q):
        y_copy(last, q, R - 1, row_from(R - 1)).wait_recv()
    for a in range(A):
        last_block(row_from(R - 1), a)
        zs[a] = csum[a].astype(BF16)
        each(1, L, lambda k: lrs_copy(a, k).start())

    def layer_sum(a):
        def add_layer(k, total):
            lrs_copy(a, k).wait_recv()
            return total + zr[a, k].astype(F32)

        return loop(1, L, add_layer, csum[a, layer])

    for slot in range(AP):
        need(LP + A * T + slot)
    for a in range(A):
        residual = arhs_t[a, layer] - layer_sum(a)
        for s in range(a):

            def add_block(k, total):
                source = row_from(k)
                if s == a - 1:
                    z_copy(s, k, source).wait_recv()
                return total - dot(zbuf[s, source], top_m[pair_index(a, s), source], NT)

            residual = residual - dot(zbuf[s, row], top_m[pair_index(a, s), row], NT)
            residual = loop(1, R, add_block, residual)
        zbuf[a, row] = solve(ainv, a, residual, False).astype(BF16)
        if a < A - 1:
            each(1, R, lambda k: z_copy(a, R - k, row).start())
    for a in range(A - 1, -1, -1):
        residual = zbuf[a, row].astype(F32)
        if a < A - 1:

            def partial(target):
                total = None
                for b in range(a + 1, A):
                    term = dot(xanc[b, layer], top_m[pair_index(b, a), target], NN)
                    total = term if total is None else total + term
                return total

            def send_part(k):
                asend[a, k] = partial(row_to(k)).astype(BF16)
                a_copy(a, k).start()

            each(1, R, lambda k: send_part(R - k))

            def add_part(k, total):
                a_copy(a, k).wait_recv()
                return total + arecv[a, k].astype(F32)

            residual = residual - loop(1, R, add_part, partial(row))
        xanc[a, layer] = solve(ainv, a, residual, True).astype(BF16)
        each(1, L, lambda k: lag_copy(a, k, layer).start())

    def out_place(slot, owner):
        cols = pl.ds(pl.multiple_of(owner * H, H), H)
        return leaf_out.at[0, slot, :, cols] if slot < T else anc_out.at[slot - T, :, cols]

    def out_copy(slot, k, source):
        block = out_place(slot, source)
        return remote(
            block, block, out_ssem.at[slot, k], out_rsem.at[slot, k], "col", ahead(col, k, C)
        )

    def emit(slot, value):
        turned = value.astype(F32).T.astype(BF16)
        if slot < T:
            leaf_out[0, slot, :, my_cols] = turned
        else:
            anc_out[slot - T, :, my_cols] = turned
        for k in range(1, C):
            out_copy(slot, k, col).start()

    def anc_chunk(a, q):
        return xanc[a, pl.ds(q * LQ, LQ)].reshape(HQ, B)

    def fold_back(t, vector, tiles, first=False):
        def one(k):
            term = dot(vector, tiles(k), NN).reshape(Q, HQ, B)
            bsum[t, :, k] = term if first else bsum[t, :, k] + term

        each(0, R, one)

    def fold_cross(a, t):
        fold_back(t, xanc[a].reshape(H, B), lambda k: cross_m[a, t, k], a == A - 1)

    def start_level(t, q):
        def value(target):
            total = bsum[t, q, target]
            if t == T - 1:
                return total + dot(anc_chunk(0, q), cross_m[0, t, target], NN)
            return total + dot(xbuf[t + 1, q], leaf_m[pair_index(t + 1, t), target], NN)

        def send_part(k):
            bsend[t, q, k] = value(row_to(k)).astype(BF16)
            b_copy(t, q, k).start()

        each(1, R, lambda k: send_part(R - k))
        bown[t, q] = value(row)

    for a in range(A - 1, 0, -1):
        each(1, L, lambda k: lag_copy(a, k, behind(layer, k, L)).wait_recv())
        fold_cross(a, T - 1)
    each(1, L, lambda k: lag_copy(0, k, behind(layer, k, L)).wait_recv())
    for q in range(Q):
        start_level(T - 1, q)
    for t in range(T - 2, -1, -1):
        for a in range(A - 1, -1, -1):
            fold_cross(a, t)
    for a in range(A):
        emit(T + a, xanc[a].reshape(H, B))
    for t in range(T - 1, -1, -1):
        for q in range(Q):

            def add_part(k, total):
                b_copy(t, q, k).wait_recv()
                return total + brecv[t, q, k].astype(F32)

            residual = ybuf[t, q, row].astype(F32) - loop(1, R, add_part, bown[t, q])
            xbuf[t, q] = solve(inv, t, residual, True).astype(BF16)
            if t > 0:
                start_level(t - 1, q)
        emit(t, xbuf[t].reshape(H, B))
        for lower in range(t - 1):
            fold_back(lower, xbuf[t].reshape(H, B), lambda k: leaf_m[pair_index(t, lower), k])

    for slot in range(LP + A * T + AP):
        for k in range(1, C):
            tile_copy(slot, k, col).wait_send()
    for t in range(T):
        for q in range(Q):
            each(1, R, lambda k: y_copy(t, q, k, row).wait_send())
            each(1, R, lambda k: b_copy(t, q, k).wait_send())
    for a in range(A - 1):
        each(1, R, lambda k: z_copy(a, k, row).wait_send())
        each(1, R, lambda k: a_copy(a, k).wait_send())
    for a in range(A):
        each(1, L, lambda k: lrs_copy(a, k).wait_send())
        each(1, L, lambda k: lag_copy(a, k, layer).wait_send())
    for slot in range(T + A):
        for k in range(1, C):
            out_copy(slot, k, col).wait_send()
            out_copy(slot, k, behind(col, k, C)).wait_recv()


def local(R, L, C, *arrays):
    leaf_rhs, anc_rhs = arrays[:2]
    T = leaf_rhs.shape[1]
    A = anc_rhs.shape[0]
    B = leaf_rhs.shape[2]
    H = leaf_rhs.shape[3] // C
    W = arrays[8].shape[-1]
    Q = 1
    HQ, HL = H // Q, H // L
    SB = B // W
    LP, AP = T * (T - 1) // 2, A * (A - 1) // 2
    dims = (R, L, C, Q, T, A, B, H, HQ, HL, W)
    vmem = pltpu.VMEM
    dma = pltpu.SemaphoreType.DMA
    slots = LP + A * T + AP
    scratch = [
        vmem((T, B, H), F32), vmem((A, B, H), F32),
        vmem((T, SB, W, W), BF16), vmem((A, SB, W, W), BF16),
        vmem((T, Q, HQ, B), F32), vmem((A, L, HL, B), F32),
        vmem((LP, R, B, B), BF16), vmem((A, T, R, B, B), BF16), vmem((AP, R, B, B), BF16),
        vmem((T, Q, R, HQ, B), BF16), vmem((T, Q, HQ, B), F32), vmem((A, L, HL, B), F32),
        vmem((A, L, HL, B), BF16), vmem((A, L, HL, B), BF16),
        vmem((A, R, HL, B), BF16), vmem((A, L, HL, B), BF16),
        vmem((A, R, HL, B), BF16), vmem((A, R, HL, B), BF16),
        vmem((T, Q, R, HQ, B), F32), vmem((T, Q, HQ, B), F32),
        vmem((T, Q, R, HQ, B), BF16), vmem((T, Q, R, HQ, B), BF16),
        vmem((T, Q, HQ, B), BF16),
        dma((T + 3 + 3 * (R // C),)),
        dma((slots, C)), dma((slots, C)),
        dma((T, Q, R)), dma((T, Q, R)), dma((A, R)), dma((A, R)),
        dma((A, L)), dma((A, L)), dma((A, L)), dma((A, L)),
        dma((A, R)), dma((A, R)), dma((T, Q, R)), dma((T, Q, R)),
        dma((T + A, C)), dma((T + A, C)),
    ]
    anywhere = pl.BlockSpec(memory_space=pl.ANY)
    scalars = pl.BlockSpec(memory_space=pltpu.SMEM)
    return pl.pallas_call(
        functools.partial(kernel, dims),
        out_shape=(
            vmem(leaf_rhs.shape, BF16),
            vmem(anc_rhs.shape, BF16),
        ),
        in_specs=[anywhere] * 5 + [scalars] * 3 + [anywhere] * 2,
        out_specs=(pl.BlockSpec(memory_space=vmem),) * 2,
        scratch_shapes=scratch,
        compiler_params=pltpu.CompilerParams(
            collective_id=0, has_side_effects=True, vmem_limit_bytes=56 * 1024 * 1024
        ),
    )(*arrays)


def solution(mesh):
    in_specs = (
        P("layer", None, "row", None),
        P(None, "row", None),
        P("layer", None, "row", "col"),
        P("layer", None, None, "row", "col"),
        P(None, "row", "col"),
        P("layer", None, "row", "col"),
        P("layer", None, None, "row", "col"),
        P(None, "row", "col"),
        P("layer", None, None, None, None),
        P(),
    )
    out_specs = (P("layer", None, "row", None), P(None, "row", None))
    sizes = mesh.shape
    return jax.shard_map(
        functools.partial(local, sizes["row"], sizes["layer"], sizes["col"]),
        mesh=mesh, in_specs=in_specs, out_specs=out_specs, check_vma=False,
    )
```

```python
import functools

import jax
import jax.numpy as jnp
from jax import lax
from jax.experimental import pallas as pl
from jax.experimental.pallas import tpu as pltpu
from jax.sharding import PartitionSpec as P

MESH = pl.DeviceIdType.MESH
NT = (((1,), (1,)), ((), ()))
NN = (((1,), (0,)), ((), ()))
F32 = jnp.float32
BF16 = jnp.bfloat16


def pair_index(target, source):
    return target * (target - 1) // 2 + source


def dot(left, right, form):
    return lax.dot_general(left, right, form, preferred_element_type=F32)


def loop(start, stop, body, init):
    if stop - start <= 4:
        carry = init
        for index in range(start, stop):
            carry = body(index, carry)
        return carry
    return lax.fori_loop(start, stop, body, init)


def solve(inverse, level, residual, flipped):
    wide = inverse.shape[-1]
    pieces = []
    rounded = residual.astype(BF16)
    for block in range(inverse.shape[1]):
        part = rounded[:, block * wide : (block + 1) * wide]
        pieces.append(dot(part, inverse[level, block], NN if flipped else NT))
    return jnp.concatenate(pieces, axis=1)


def kernel(
    dims,
    leaf_rhs, anc_rhs, leaf_tiles, cross_tiles, top_tiles,
    leaf_pat, cross_pat, top_pat, leaf_inv, anc_inv,
    leaf_out, anc_out,
    rhs_in, arhs_in, inv, ainv, rhs_t, arhs_t, leaf_m, cross_m, top_m,
    ybuf, fsum, csum, zs, zr, zbuf, xanc, asend, arecv,
    bsum, bown, bsend, brecv, xbuf,
    load_sem, col_ssem, col_rsem, y_ssem, y_rsem, z_ssem, z_rsem,
    lrs_ssem, lrs_rsem, lag_ssem, lag_rsem, a_ssem, a_rsem, b_ssem, b_rsem,
    out_ssem, out_rsem,
):
    R, L, C, Q, T, A, B, H, HQ, HL, W = dims
    RC = R // C
    LQ = L // Q
    SB = B // W
    LP = T * (T - 1) // 2
    AP = A * (A - 1) // 2
    row = lax.axis_index("row")
    layer = lax.axis_index("layer")
    col = lax.axis_index("col")

    def ahead(axis_index, step, size):
        return lax.rem(axis_index + step, size)

    def behind(axis_index, step, size):
        return lax.rem(axis_index + size - step, size)

    binary = R & (R - 1) == 0

    def row_to(step):
        if not binary:
            return ahead(row, step, R)
        total, place = 0, 1
        while place < R:
            total = total + lax.rem(lax.div(row, place) + step // place, 2) * place
            place *= 2
        return total

    def row_from(step):
        return row_to(step) if binary else behind(row, step, R)

    loads = []

    def load(src, dst):
        copy = pltpu.make_async_copy(src, dst, load_sem.at[len(loads)])
        copy.start()
        loads.append(copy)
        return copy

    my_cols = pl.ds(pl.multiple_of(col * H, H), H)
    ld_rhs = [load(leaf_rhs.at[0, 0, :, my_cols], rhs_in.at[0])]
    ld_inv = load(leaf_inv.at[0, :, pl.ds(row * SB, SB)], inv)
    barrier = pltpu.get_barrier_semaphore()
    for name, mine, size in (("row", row, R), ("layer", layer, L), ("col", col, C)):
        for step in range(1, size):
            pl.semaphore_signal(
                barrier, inc=1, device_id={name: ahead(mine, step, size)}, device_id_type=MESH
            )

    ld_leaf = [
        load(leaf_tiles.at[0, :, :, pl.ds(j * B, B)], leaf_m.at[:, col * RC + j])
        for j in range(RC)
    ]
    for t in range(1, T):
        ld_rhs.append(load(leaf_rhs.at[0, t, :, my_cols], rhs_in.at[t]))
    ld_cross = [
        load(cross_tiles.at[0, :, :, :, pl.ds(j * B, B)], cross_m.at[:, :, col * RC + j])
        for j in range(RC)
    ]
    ld_top = [
        load(top_tiles.at[:, :, pl.ds(j * B, B)], top_m.at[:, col * RC + j])
        for j in range(RC)
    ]
    ld_arhs = load(anc_rhs.at[:, :, my_cols], arhs_in)
    ld_ainv = load(anc_inv.at[:, pl.ds(row * SB, SB)], ainv)

    def remote(src, dst, ssem, rsem, name, target):
        return pltpu.make_async_remote_copy(
            src_ref=src, dst_ref=dst, send_sem=ssem, recv_sem=rsem,
            device_id={name: target}, device_id_type=MESH,
        )

    def y_copy(t, q, k, source):
        block = ybuf.at[t, q, source]
        return remote(block, block, y_ssem.at[t, q, k], y_rsem.at[t, q, k], "row", row_to(k))

    def z_copy(a, k, source):
        block = zbuf.at[a, source]
        return remote(block, block, z_ssem.at[a, k], z_rsem.at[a, k], "row", row_to(k))

    def a_copy(a, k):
        return remote(
            asend.at[a, k], arecv.at[a, k], a_ssem.at[a, k], a_rsem.at[a, k], "row", row_to(k)
        )

    def b_copy(t, q, k):
        return remote(
            bsend.at[t, q, k], brecv.at[t, q, k], b_ssem.at[t, q, k], b_rsem.at[t, q, k],
            "row", row_to(k),
        )

    def lrs_copy(a, k):
        target = ahead(layer, k, L)
        return remote(
            zs.at[a, target], zr.at[a, k], lrs_ssem.at[a, k], lrs_rsem.at[a, k], "layer", target
        )

    def lag_copy(a, k, source):
        block = xanc.at[a, source]
        return remote(
            block, block, lag_ssem.at[a, k], lag_rsem.at[a, k], "layer", ahead(layer, k, L)
        )

    def tile_copy(slot, k, source):
        held = pl.ds(source * RC, RC)
        if slot < LP:
            block = leaf_m.at[slot, held]
        elif slot < LP + A * T:
            block = cross_m.at[(slot - LP) // T, (slot - LP) % T, held]
        else:
            block = top_m.at[slot - LP - A * T, held]
        return remote(
            block, block, col_ssem.at[slot, k], col_rsem.at[slot, k], "col", ahead(col, k, C)
        )

    def tiles_arrive(slot):
        for k in range(1, C):
            tile_copy(slot, k, behind(col, k, C)).wait_recv()

    def send_tiles(slot):
        for k in range(1, C):
            tile_copy(slot, k, col).start()

    def each(start, stop, action):
        def body(index, carry):
            action(index)
            return carry

        loop(start, stop, body, 0)

    def mask(ref, lead, pattern, lead_pattern):
        def one(j):
            for i in range(SB):
                for n in range(SB):
                    bit = pattern[(*lead_pattern, i, j * SB + n)].astype(F32)
                    spread = jnp.full((W, W), bit, F32).astype(BF16)
                    at = (*lead, col * RC + j, pl.ds(i * W, W), pl.ds(n * W, W))
                    ref[at] = ref[at] * spread

        each(0, RC, one)

    def send_y(t, q):
        each(1, R, lambda k: y_copy(t, q, R - k, row).start())

    def turn_rhs(t):
        ld_rhs[t].wait()
        rhs_t[t] = rhs_in[t].T.reshape(Q, HQ, B)

    turn_rhs(0)
    ld_inv.wait()
    for q in range(Q):
        ybuf[0, q, row] = solve(inv, 0, rhs_t[0, q], False).astype(BF16)
    pl.semaphore_wait(barrier, (R - 1) + (L - 1) + (C - 1))
    for q in range(Q):
        send_y(0, q)
    for copy in ld_leaf:
        copy.wait()
    for slot in range(LP):
        mask(leaf_m, (slot,), leaf_pat, (0, slot))
        send_tiles(slot)
    for t in range(1, T):
        turn_rhs(t)
    def prepare_cross():
        for copy in ld_cross:
            copy.wait()
        for t in range(T):
            for a in range(A):
                mask(cross_m, (a, t), cross_pat, (0, a, t))
                send_tiles(LP + a * T + t)

    def prepare_top():
        for copy in ld_top:
            copy.wait()
        for slot in range(AP):
            mask(top_m, (slot,), top_pat, (slot,))
            send_tiles(LP + A * T + slot)
        ld_arhs.wait()
        ld_ainv.wait()
        for a in range(A):
            arhs_t[a] = arhs_in[a].T.reshape(L, HL, B)

    def product(vectors, tiles, form=NT):
        return loop(
            1, R,
            lambda k, total: total + dot(vectors(k), tiles(k), form),
            dot(vectors(0), tiles(0), form),
        )

    arrived = set()

    def need(slot):
        if slot not in arrived:
            arrived.add(slot)
            tiles_arrive(slot)

    def whole(ref, lead, k):
        return ref[(lead, slice(None), k)].reshape(H, B)

    def fold_leaf(s):
        for t in range(s + 2, T):
            need(pair_index(t, s))
            term = product(lambda k: whole(ybuf, s, k), lambda k: leaf_m[pair_index(t, s), k])
            term = term.reshape(Q, HQ, B)
            fsum[t] = term if s == 0 else fsum[t] + term

    def fold_ancestor(s, a):
        need(LP + a * T + s)
        term = product(lambda k: whole(ybuf, s, k), lambda k: cross_m[a, s, k])
        term = term.reshape(L, HL, B)
        csum[a] = term if s == 0 else csum[a] + term

    for t in range(1, T):
        for q in range(Q):
            need(pair_index(t, t - 1))

            def arriving(k, total):
                source = row_from(k)
                y_copy(t - 1, q, k, source).wait_recv()
                return total + dot(ybuf[t - 1, q, source], leaf_m[pair_index(t, t - 1), source], NT)

            residual = rhs_t[t, q]
            if t > 1:
                residual = residual - fsum[t, q]
            own = dot(ybuf[t - 1, q, row], leaf_m[pair_index(t, t - 1), row], NT)
            residual = residual - loop(1, R, arriving, own)
            ybuf[t, q, row] = solve(inv, t, residual, False).astype(BF16)
            send_y(t, q)
        fold_leaf(t - 1)
        if t == 1:
            prepare_cross()
        if t == T - 1:
            prepare_top()
            for s in range(t):
                for a in range(A):
                    fold_ancestor(s, a)

    last = T - 1
    for a in range(A):
        need(LP + a * T + last)

    def last_block(source, a):
        term = dot(whole(ybuf, last, source), cross_m[a, last, source], NT)
        csum[a] += term.reshape(L, HL, B)

    for a in range(A):
        last_block(row, a)

    def last_arrival(k):
        for q in range(Q):
            y_copy(last, q, k, row_from(k)).wait_recv()
        for a in range(A):
            last_block(row_from(k), a)

    each(1, R - 1, last_arrival)
    for q in range(Q):
        y_copy(last, q, R - 1, row_from(R - 1)).wait_recv()
    for a in range(A):
        last_block(row_from(R - 1), a)
        zs[a] = csum[a].astype(BF16)
        each(1, L, lambda k: lrs_copy(a, k).start())

    def layer_sum(a):
        def add_layer(k, total):
            lrs_copy(a, k).wait_recv()
            return total + zr[a, k].astype(F32)

        return loop(1, L, add_layer, csum[a, layer])

    for slot in range(AP):
        need(LP + A * T + slot)
    for a in range(A):
        residual = arhs_t[a, layer] - layer_sum(a)
        for s in range(a):

            def add_block(k, total):
                source = row_from(k)
                if s == a - 1:
                    z_copy(s, k, source).wait_recv()
                return total - dot(zbuf[s, source], top_m[pair_index(a, s), source], NT)

            residual = residual - dot(zbuf[s, row], top_m[pair_index(a, s), row], NT)
            residual = loop(1, R, add_block, residual)
        zbuf[a, row] = solve(ainv, a, residual, False).astype(BF16)
        if a < A - 1:
            each(1, R, lambda k: z_copy(a, R - k, row).start())
    for a in range(A - 1, -1, -1):
        residual = zbuf[a, row].astype(F32)
        if a < A - 1:

            def partial(target):
                total = None
                for b in range(a + 1, A):
                    term = dot(xanc[b, layer], top_m[pair_index(b, a), target], NN)
                    total = term if total is None else total + term
                return total

            def send_part(k):
                asend[a, k] = partial(row_to(k)).astype(BF16)
                a_copy(a, k).start()

            each(1, R, lambda k: send_part(R - k))

            def add_part(k, total):
                a_copy(a, k).wait_recv()
                return total + arecv[a, k].astype(F32)

            residual = residual - loop(1, R, add_part, partial(row))
        xanc[a, layer] = solve(ainv, a, residual, True).astype(BF16)
        each(1, L, lambda k: lag_copy(a, k, layer).start())

    def out_place(slot, owner):
        cols = pl.ds(pl.multiple_of(owner * H, H), H)
        return leaf_out.at[0, slot, :, cols] if slot < T else anc_out.at[slot - T, :, cols]

    def out_copy(slot, k, source):
        block = out_place(slot, source)
        return remote(
            block, block, out_ssem.at[slot, k], out_rsem.at[slot, k], "col", ahead(col, k, C)
        )

    def emit(slot, value):
        turned = value.astype(F32).T.astype(BF16)
        if slot < T:
            leaf_out[0, slot, :, my_cols] = turned
        else:
            anc_out[slot - T, :, my_cols] = turned
        for k in range(1, C):
            out_copy(slot, k, col).start()

    def anc_chunk(a, q):
        return xanc[a, pl.ds(q * LQ, LQ)].reshape(HQ, B)

    def fold_back(t, vector, tiles, first=False):
        def one(k):
            term = dot(vector, tiles(k), NN).reshape(Q, HQ, B)
            bsum[t, :, k] = term if first else bsum[t, :, k] + term

        each(0, R, one)

    def fold_ancestors(t, source=None):
        def one(k):
            term = None
            for a in range(A):
                more = dot(xanc[a].reshape(H, B), cross_m[a, t, k], NN)
                term = more if term is None else term + more
            if source is not None:
                term = term + dot(xbuf[source].reshape(H, B), leaf_m[pair_index(source, t), k], NN)
            bsum[t, :, k] = term.reshape(Q, HQ, B)

        each(0, R, one)

    def fold_cross(a, t):
        fold_back(t, xanc[a].reshape(H, B), lambda k: cross_m[a, t, k], a == A - 1)

    def start_level(t, q):
        def value(target):
            total = bsum[t, q, target]
            if t == T - 1:
                return total + dot(anc_chunk(0, q), cross_m[0, t, target], NN)
            return total + dot(xbuf[t + 1, q], leaf_m[pair_index(t + 1, t), target], NN)

        def send_part(k):
            bsend[t, q, k] = value(row_to(k)).astype(BF16)
            b_copy(t, q, k).start()

        each(1, R, lambda k: send_part(R - k))
        bown[t, q] = value(row)

    for a in range(A - 1, 0, -1):
        each(1, L, lambda k: lag_copy(a, k, behind(layer, k, L)).wait_recv())
        fold_cross(a, T - 1)
    each(1, L, lambda k: lag_copy(0, k, behind(layer, k, L)).wait_recv())
    for q in range(Q):
        start_level(T - 1, q)
    if T > 1:
        fold_ancestors(T - 2)
    for t in range(T - 1, -1, -1):
        for q in range(Q):

            def add_part(k, total):
                b_copy(t, q, k).wait_recv()
                return total + brecv[t, q, k].astype(F32)

            residual = ybuf[t, q, row].astype(F32) - loop(1, R, add_part, bown[t, q])
            xbuf[t, q] = solve(inv, t, residual, True).astype(BF16)
            if t > 0:
                start_level(t - 1, q)
        if t > 1:
            fold_ancestors(t - 2, t)
            for upper in range(t + 1, T):
                fold_back(
                    t - 2, xbuf[upper].reshape(H, B), lambda k: leaf_m[pair_index(upper, t - 2), k]
                )
        emit(t, xbuf[t].reshape(H, B))
        if t == min(1, T - 1):
            for a in range(A):
                emit(T + a, xanc[a].reshape(H, B))

    for slot in range(LP + A * T + AP):
        for k in range(1, C):
            tile_copy(slot, k, col).wait_send()
    for t in range(T):
        for q in range(Q):
            each(1, R, lambda k: y_copy(t, q, k, row).wait_send())
            each(1, R, lambda k: b_copy(t, q, k).wait_send())
    for a in range(A - 1):
        each(1, R, lambda k: z_copy(a, k, row).wait_send())
        each(1, R, lambda k: a_copy(a, k).wait_send())
    for a in range(A):
        each(1, L, lambda k: lrs_copy(a, k).wait_send())
        each(1, L, lambda k: lag_copy(a, k, layer).wait_send())
    for slot in range(T + A):
        for k in range(1, C):
            out_copy(slot, k, col).wait_send()
            out_copy(slot, k, behind(col, k, C)).wait_recv()


def write_out(leaf_in, anc_in, leaf_out, anc_out, sems):
    copies = [
        pltpu.make_async_copy(leaf_in, leaf_out, sems.at[0]),
        pltpu.make_async_copy(anc_in, anc_out, sems.at[1]),
    ]
    for copy in copies:
        copy.start()
    for copy in copies:
        copy.wait()


def local(R, L, C, *arrays):
    leaf_rhs, anc_rhs = arrays[:2]
    T = leaf_rhs.shape[1]
    A = anc_rhs.shape[0]
    B = leaf_rhs.shape[2]
    H = leaf_rhs.shape[3] // C
    W = arrays[8].shape[-1]
    Q = 2 if R <= 4 and L % 2 == 0 else 1
    HQ, HL = H // Q, H // L
    SB = B // W
    LP, AP = T * (T - 1) // 2, A * (A - 1) // 2
    dims = (R, L, C, Q, T, A, B, H, HQ, HL, W)
    vmem = pltpu.VMEM
    dma = pltpu.SemaphoreType.DMA
    slots = LP + A * T + AP
    scratch = [
        vmem((T, B, H), F32), vmem((A, B, H), F32),
        vmem((T, SB, W, W), BF16), vmem((A, SB, W, W), BF16),
        vmem((T, Q, HQ, B), F32), vmem((A, L, HL, B), F32),
        vmem((LP, R, B, B), BF16), vmem((A, T, R, B, B), BF16), vmem((AP, R, B, B), BF16),
        vmem((T, Q, R, HQ, B), BF16), vmem((T, Q, HQ, B), F32), vmem((A, L, HL, B), F32),
        vmem((A, L, HL, B), BF16), vmem((A, L, HL, B), BF16),
        vmem((A, R, HL, B), BF16), vmem((A, L, HL, B), BF16),
        vmem((A, R, HL, B), BF16), vmem((A, R, HL, B), BF16),
        vmem((T, Q, R, HQ, B), F32), vmem((T, Q, HQ, B), F32),
        vmem((T, Q, R, HQ, B), BF16), vmem((T, Q, R, HQ, B), BF16),
        vmem((T, Q, HQ, B), BF16),
        dma((T + 3 + 3 * (R // C),)),
        dma((slots, C)), dma((slots, C)),
        dma((T, Q, R)), dma((T, Q, R)), dma((A, R)), dma((A, R)),
        dma((A, L)), dma((A, L)), dma((A, L)), dma((A, L)),
        dma((A, R)), dma((A, R)), dma((T, Q, R)), dma((T, Q, R)),
        dma((T + A, C)), dma((T + A, C)),
    ]
    anywhere = pl.BlockSpec(memory_space=pl.ANY)
    scalars = pl.BlockSpec(memory_space=pltpu.SMEM)
    solved = pl.pallas_call(
        functools.partial(kernel, dims),
        out_shape=(
            vmem(leaf_rhs.shape, BF16),
            vmem(anc_rhs.shape, BF16),
        ),
        in_specs=[anywhere] * 5 + [scalars] * 3 + [anywhere] * 2,
        out_specs=(pl.BlockSpec(memory_space=vmem),) * 2,
        scratch_shapes=scratch,
        compiler_params=pltpu.CompilerParams(
            collective_id=0, has_side_effects=True, vmem_limit_bytes=56 * 1024 * 1024
        ),
    )(*arrays)
    return pl.pallas_call(
        write_out,
        out_shape=(
            jax.ShapeDtypeStruct(leaf_rhs.shape, BF16),
            jax.ShapeDtypeStruct(anc_rhs.shape, BF16),
        ),
        in_specs=[pl.BlockSpec(memory_space=vmem)] * 2,
        out_specs=(anywhere, anywhere),
        scratch_shapes=[dma((2,))],
    )(*solved)


def solution(mesh):
    in_specs = (
        P("layer", None, "row", None),
        P(None, "row", None),
        P("layer", None, "row", "col"),
        P("layer", None, None, "row", "col"),
        P(None, "row", "col"),
        P("layer", None, "row", "col"),
        P("layer", None, None, "row", "col"),
        P(None, "row", "col"),
        P("layer", None, None, None, None),
        P(),
    )
    out_specs = (P("layer", None, "row", None), P(None, "row", None))
    sizes = mesh.shape
    return jax.shard_map(
        functools.partial(local, sizes["row"], sizes["layer"], sizes["col"]),
        mesh=mesh, in_specs=in_specs, out_specs=out_specs, check_vma=False,
    )
```
